128 devices in a mesh: px: 8 (over x, core), py: 16 (over y, z).
Axes of the slice: x: 4, y: 4, z: 4, core: 2. Of those that a mesh axis runs over, the one named last changes fastest.
Arguments:
- feats: bfloat16 [65536, 256], P(('px', 'py')), may hold values from -6 to 6
- stale_feats: bfloat16 [65536, 256], P(('px', 'py')), may hold values from -6 to 6
- local_adj: bfloat16 [65536, 512], P(('px', 'py')), may hold values from -0.046875 to 0.046875
- adj_in: bfloat16 [16384, 128, 128], P(('px', 'py')), may hold values from -0.046875 to 0.046875
- adj_out: bfloat16 [16384, 128, 128], P(('px', 'py')), may hold values from -0.046875 to 0.046875
- owner: int32 [128, 128], replicated, may hold values from 0 to 1, as said below
- send_idx: int32 [16384, 128], P(('px', 'py')), may hold values from 0 to 511
- recv_idx: int32 [16384, 128], P(('px', 'py')), may hold values from 0 to 511
- weight: bfloat16 [256, 256], replicated, may hold values from -0.375 to 0.375
- cotangent: bfloat16 [65536, 256], P(('px', 'py'))
Outputs:
- out_feats: bfloat16 [65536, 256], P(('px', 'py'))
- feat_grad: bfloat16 [65536, 256], P(('px', 'py'))
- bound_grad: bfloat16 [65536, 256], P(('px', 'py'))
- weight_grad: float32 [256, 256], replicated
The draws below stay inside these ranges and needn't reach their ends.
Inputs may be any that keep to these rules, and one draw needn't show every extreme that they name: `owner`: the diagonal is unused.
All inputs are finite; a program needn't handle non-finite values.
Results may differ from the reference program's by a relative error of at most 0.0085.
Values may be sent and summed in bfloat16 or wider, within the bound.
A program may use at most 128 MiB of HBM per device.

```python
import jax
import jax.numpy as jnp
from jax import lax

FEAT = 256
ROWS_DEV = 512
SLOT = 128
ALL_ROWS = 65536
PAIRS = 16384
DEVICES = 128


def draw_owner(key, part):
    key = jax.random.fold_in(key, 11)
    load_key, pick_key = jax.random.split(key)
    loads = jax.random.randint(load_key, (DEVICES, 1), 1, 10)
    picks = jax.random.randint(pick_key, (DEVICES, DEVICES), 0, 10)
    return (picks < loads).astype(jnp.int32)


def draw_cotangent(key, part):
    key = jax.random.fold_in(key, 23)
    rows = jnp.arange(ALL_ROWS) // ROWS_DEV
    factor = 1.0 + 2.0 * rows.astype(jnp.float32) / max(DEVICES - 1, 1)
    values = jax.random.normal(key, (ALL_ROWS, FEAT), jnp.float32)
    return (values * factor[:, None]).astype(jnp.bfloat16)


def with_ends(result, own_key, least, largest):
    longest = result.shape.index(max(result.shape))
    spots = []
    for shift in (0, 1):
        where = [jax.random.randint(jax.random.fold_in(own_key, axis), (), 0, length) for axis, length in enumerate(result.shape)]
        where[longest] = (where[longest] + shift) % result.shape[longest]
        spots.append(tuple(where))
    return result.at[spots[0]].set(least).at[spots[1]].set(largest)


def levels(rng, shape, pieces, smallest, top_value):
    factor_of, own = 1.0, jax.random.fold_in(rng, 6)
    for dim, parts in pieces:
        draws = jnp.exp(jax.random.uniform(jax.random.fold_in(own, dim), (parts,), jnp.float32, smallest / len(pieces), top_value / len(pieces)))
        factor_of = factor_of * jnp.repeat(draws, shape[dim] // parts).reshape([-1 if axis == dim else 1 for axis in range(len(shape))])
    return factor_of


def gaussian(rng, shape, deviation, most, cuts=(), kind=jnp.bfloat16):
    array = deviation * jax.random.normal(rng, shape, jnp.float32)
    if cuts:
        array = array * levels(rng, shape, cuts, -0.22, 0.18)
    return jnp.clip(array, -most, most).astype(kind)


def setup_inputs(seed: int = 0) -> dict:
    key_list = jax.random.split(jax.random.key(seed), 11)
    feats = gaussian(key_list[0], (ALL_ROWS, FEAT), 1.0, 6.0, ((0, 128),))
    stale_feats = gaussian(key_list[1], (ALL_ROWS, FEAT), 1.0, 6.0, ((0, 128),))
    local_adj = gaussian(key_list[2], (ALL_ROWS, ROWS_DEV), (ROWS_DEV + DEVICES * SLOT) ** -0.5, 0.046875, ((0, 128),))
    adj_in = gaussian(key_list[3], (PAIRS, SLOT, SLOT), (ROWS_DEV + DEVICES * SLOT) ** -0.5, 0.046875, ((0, 128),))
    adj_out = gaussian(key_list[4], (PAIRS, SLOT, SLOT), (ROWS_DEV + DEVICES * SLOT) ** -0.5, 0.046875, ((0, 128),))
    owner = draw_owner(jax.random.fold_in(key_list[10], 71), 0)
    send_idx = with_ends(jax.random.randint(key_list[6], (PAIRS, SLOT), 0, ROWS_DEV), jax.random.fold_in(key_list[6], 1), 0, ROWS_DEV - 1).astype(jnp.int32)
    recv_idx = with_ends(jax.random.randint(key_list[7], (PAIRS, SLOT), 0, ROWS_DEV), jax.random.fold_in(key_list[7], 1), 0, ROWS_DEV - 1).astype(jnp.int32)
    weight = gaussian(key_list[8], (FEAT, FEAT), FEAT ** -0.5, 0.375)
    cotangent = draw_cotangent(jax.random.fold_in(key_list[10], 71), 0)
    return {"feats": feats, "stale_feats": stale_feats, "local_adj": local_adj, "adj_in": adj_in, "adj_out": adj_out, "owner": owner, "send_idx": send_idx, "recv_idx": recv_idx, "weight": weight, "cotangent": cotangent}


def gelu_grad(pre, grad):
    return jax.vjp(jax.nn.gelu, pre)[1](grad)[0]

def reference(feats, stale_feats, local_adj, adj_in, adj_out, owner, send_idx, recv_idx, weight, cotangent):
    feat_all = feats.reshape(DEVICES, ROWS_DEV, FEAT)
    stale_all = stale_feats.reshape(DEVICES, ROWS_DEV, FEAT)
    local_all = local_adj.reshape(DEVICES, ROWS_DEV, ROWS_DEV)
    tiles_in = adj_in.reshape(DEVICES, DEVICES, SLOT, SLOT)
    tiles_out = adj_out.reshape(DEVICES, DEVICES, SLOT, SLOT)
    send_all = send_idx.reshape(DEVICES, DEVICES, SLOT)
    recv_all = recv_idx.reshape(DEVICES, DEVICES, SLOT)
    grad_all = cotangent.reshape(DEVICES, ROWS_DEV, FEAT)
    peer_ids = jnp.arange(DEVICES, dtype=jnp.int32)

    def tiles_for(dest):
        chosen = owner[dest][:, None, None] == 1
        return jnp.where(chosen, tiles_in[dest], tiles_out[:, dest])

    def forward_one(dest):
        tiles = tiles_for(dest)
        rows = jnp.take_along_axis(stale_all, send_all[:, dest][:, :, None], axis=1)
        pair_sum = jnp.einsum('qij,qjf->qif', tiles.astype(jnp.float32), rows.astype(jnp.float32)).astype(jnp.bfloat16)
        pair_sum = jnp.where((peer_ids == dest)[:, None, None], jnp.zeros_like(pair_sum), pair_sum)
        total = jnp.dot(local_all[dest], feat_all[dest], preferred_element_type=jnp.float32)
        total = total.at[recv_all[dest].reshape(-1)].add(pair_sum.reshape(-1, FEAT).astype(jnp.float32))
        summed = total.astype(jnp.bfloat16)
        pre = jnp.dot(summed, weight, preferred_element_type=jnp.float32)
        output = jax.nn.gelu(pre).astype(jnp.bfloat16)
        pre_grad = gelu_grad(pre, grad_all[dest].astype(jnp.float32)).astype(jnp.bfloat16)
        w_term = jnp.dot(summed.T, pre_grad, preferred_element_type=jnp.float32)
        summed_grad = jnp.dot(pre_grad, weight.T, preferred_element_type=jnp.float32).astype(jnp.bfloat16)
        local_grad = jnp.dot(local_all[dest].T, summed_grad, preferred_element_type=jnp.float32).astype(jnp.bfloat16)
        return (output, local_grad, summed_grad, w_term)
    outputs, local_grads, summed_grads, w_terms = lax.map(forward_one, peer_ids)

    def backward_one(source):
        chosen = owner[:, source][:, None, None] == 1
        tiles = jnp.where(chosen, tiles_in[:, source], tiles_out[source])
        rows = jnp.take_along_axis(summed_grads, recv_all[:, source][:, :, None], axis=1)
        pair_grad = jnp.einsum('pij,pif->pjf', tiles.astype(jnp.float32), rows.astype(jnp.float32)).astype(jnp.bfloat16)
        pair_grad = jnp.where((peer_ids == source)[:, None, None], jnp.zeros_like(pair_grad), pair_grad)
        total = jnp.zeros((ROWS_DEV, FEAT), jnp.float32)
        total = total.at[send_all[source].reshape(-1)].add(pair_grad.reshape(-1, FEAT).astype(jnp.float32))
        return total.astype(jnp.bfloat16)
    bound = lax.map(backward_one, peer_ids)
    weight_grad = lax.optimization_barrier(jnp.sum(w_terms, axis=0)) / jnp.sqrt(jnp.float32(ALL_ROWS))
    return (outputs.reshape(ALL_ROWS, FEAT), local_grads.reshape(ALL_ROWS, FEAT), bound.reshape(ALL_ROWS, FEAT), weight_grad)
```

```python
import jax
import jax.numpy as jnp
from jax import lax
from jax.sharding import PartitionSpec as P

F32 = jnp.float32
BF16 = jnp.bfloat16


def gelu_grad(pre, grad):
    return jax.vjp(jax.nn.gelu, pre)[1](grad)[0]


def select_table(indices, row_count):
    positions = jnp.arange(row_count, dtype=jnp.int32)
    return (indices[..., None] == positions).astype(BF16)


def on_device(
    feats, stale_feats, local_adj, adj_in, adj_out, owner, send_idx, recv_idx, weight, cotangent
):
    nx, ny = lax.axis_size("px"), lax.axis_size("py")
    ax, ay = lax.axis_index("px"), lax.axis_index("py")
    rows, width = feats.shape
    slot = adj_in.shape[-1]

    def from_p(x):
        x = x.reshape(nx, ny, *x.shape[1:])
        return lax.all_to_all(x, "py", split_axis=1, concat_axis=1, tiled=True)

    def from_q(x):
        x = x.reshape(nx, ny, *x.shape[1:])
        return lax.all_to_all(x, "px", split_axis=0, concat_axis=0, tiled=True)

    blocks_in = from_p(adj_in)
    blocks_out = from_q(adj_out)
    recv = from_p(recv_idx)
    send = from_q(send_idx)
    stale = lax.all_gather(stale_feats, "px", axis=0)

    table = owner.reshape(nx, ny, nx, ny)
    owned = lax.dynamic_index_in_dim(table, ax, 0, keepdims=False)
    owned = lax.dynamic_index_in_dim(owned, ay, 2, keepdims=False).T
    same = (jnp.arange(nx)[:, None] == ax) & (jnp.arange(ny)[None, :] == ay)
    blocks = jnp.where((owned == 1)[:, :, None, None], blocks_in, blocks_out)
    blocks = jnp.where(same[:, :, None, None], jnp.zeros_like(blocks), blocks)
    send_hot = select_table(send, rows)
    recv_hot = select_table(recv, rows)

    boundary = jnp.einsum("ijsr,irf->ijsf", send_hot, stale, preferred_element_type=F32).astype(BF16)
    pair_sum = jnp.einsum("ijst,ijtf->ijsf", blocks, boundary, preferred_element_type=F32).astype(BF16)
    part = jnp.einsum("ijsr,ijsf->jrf", recv_hot, pair_sum, preferred_element_type=F32).astype(BF16)
    parts = lax.all_to_all(part, "py", split_axis=0, concat_axis=0, tiled=True)
    total = jnp.dot(local_adj, feats, preferred_element_type=F32) + jnp.sum(parts.astype(F32), axis=0)

    summed = total.astype(BF16)
    pre = jnp.dot(summed, weight, preferred_element_type=F32)
    out_feats = jax.nn.gelu(pre).astype(BF16)
    pre_grad = gelu_grad(pre, cotangent.astype(F32)).astype(BF16)
    summed_grad = jnp.dot(pre_grad, weight.T, preferred_element_type=F32).astype(BF16)
    grads = lax.all_gather(summed_grad, "py", axis=0)

    w_term = jnp.dot(summed.T, pre_grad, preferred_element_type=F32)
    weight_grad = lax.psum(w_term, ("px", "py")) / jnp.sqrt(F32(rows * nx * ny))
    feat_grad = jnp.dot(local_adj.T, summed_grad, preferred_element_type=F32).astype(BF16)

    back_rows = jnp.einsum("ijsr,jrf->ijsf", recv_hot, grads, preferred_element_type=F32).astype(BF16)
    pair_grad = jnp.einsum("ijst,ijsf->ijtf", blocks, back_rows, preferred_element_type=F32).astype(BF16)
    bound = jnp.einsum("ijsr,ijsf->irf", send_hot, pair_grad, preferred_element_type=F32).astype(BF16)
    bounds = lax.all_to_all(bound, "px", split_axis=0, concat_axis=0, tiled=True)
    bound_grad = jnp.sum(bounds.astype(F32), axis=0).astype(BF16)
    return (out_feats, feat_grad, bound_grad, weight_grad)


def solution(mesh):
    both = ("px", "py")
    in_specs = (
        P(both, None),
        P(both, None),
        P(both, None),
        P(both, None, None),
        P(both, None, None),
        P(),
        P(both, None),
        P(both, None),
        P(),
        P(both, None),
    )
    out_specs = (P(both, None), P(both, None), P(both, None), P())
    return jax.shard_map(
        on_device, mesh=mesh, in_specs=in_specs, out_specs=out_specs, check_vma=False
    )
```

```python
import functools

import jax
import jax.numpy as jnp
from jax import lax
from jax.experimental import pallas as pl
from jax.experimental.pallas import tpu as pltpu
from jax.sharding import PartitionSpec as P

F32 = jnp.float32
BF16 = jnp.bfloat16
MESH = pl.DeviceIdType.MESH
PX, PY, CORES, SIDE = 8, 16, 2, 4
SLOT, ROWS, FEAT = 128, 512, 256
HALF = FEAT // 2
PART = FEAT // PY


def gelu_grad(pre, grad):
    return jax.vjp(jax.nn.gelu, pre)[1](grad)[0]


def dot(left, right, left_dim=1, right_dim=0):
    return lax.dot_general(
        left, right, (((left_dim,), (right_dim,)), ((), ())), preferred_element_type=F32
    )


def hot_rows(index):
    column = jnp.broadcast_to(index.astype(F32), (SLOT, SLOT)).T
    lane = lax.broadcasted_iota(jnp.int32, (SLOT, SLOT), 1).astype(F32)
    return jnp.concatenate(
        [jnp.where(column == lane + F32(t * SLOT), 1.0, 0.0).astype(BF16) for t in range(ROWS // SLOT)],
        axis=1,
    )


def hot_columns(index, first, count):
    row = lax.broadcasted_iota(jnp.int32, (count, SLOT), 0) + first
    return jnp.where(row == index, 1.0, 0.0).astype(BF16)


def kernel(
    adj_in, adj_out, stale, send_idx, recv_idx, owner, feats, local_adj, weight, cotangent,
    out_feats, feat_grad, bound_grad, weight_grad,
    a_in, a_out, stale_all, send_all, recv_all, rows_buf, sums_buf, part_z, part_y, recv_z, recv_y,
    send_z2, send_y2, recv_z2, recv_y2, total, g_z, g_y, bound_core, bound_x, recv_core, recv_x,
    w_term, w_parts, w_sum, w_parts2, w_all,
    s_ridx, r_ridx, s_sidx, r_sidx, s_stale, r_stale, s_fwd, s_out, r_out, s_in, r_in,
    s_z, r_z, s_y, r_y, s_z2, r_z2, s_y2, r_y2,
    s_gz, r_gz, s_gy, r_gy, s_core, r_core, s_x, r_x, s_w, r_w, s_w2, r_w2, s_w3, r_w3,
):
    a, b = lax.axis_index("px"), lax.axis_index("py")
    x, c = a // CORES, a % CORES
    y, z = b // SIDE, b % SIDE
    other = 1 - c

    def at_px(to):
        return (to, b)

    def at_py(to_y, to_z):
        return (a, to_y * SIDE + to_z)

    def send(src, dst, s_sem, r_sem, to):
        pltpu.make_async_remote_copy(
            src_ref=src, dst_ref=dst, send_sem=s_sem, recv_sem=r_sem, device_id=to, device_id_type=MESH
        ).start()

    def keep(src, dst, sem):
        pltpu.make_async_copy(src, dst, sem).start()

    def wait(ref, sem):
        pltpu.make_async_copy(ref, ref, sem).wait()

    barrier = pltpu.get_barrier_semaphore()

    def greet_px(t, _):
        pl.semaphore_signal(barrier, inc=1, device_id=at_px((a + t) % PX), device_id_type=MESH)
        return 0

    def greet_py(t, _):
        to = (b + t) % PY
        pl.semaphore_signal(barrier, inc=1, device_id=(a, to), device_id_type=MESH)
        return 0

    lax.fori_loop(1, PX, greet_px, 0)
    lax.fori_loop(1, PY, greet_py, 0)
    pl.semaphore_wait(barrier, PX - 1 + PY - 1)

    keep(stale, stale_all.at[a], r_stale.at[a])
    keep(send_idx.at[a], send_all.at[a], r_sidx.at[a])
    keep(recv_idx.at[b], recv_all.at[b], r_ridx.at[b])

    def start_stale(d, _):
        send(stale, stale_all.at[a], s_stale.at[d], r_stale.at[a], at_px((x + d) % SIDE * CORES + c))
        return 0

    def start_sidx(t, _):
        to = (a + t) % PX
        send(send_idx.at[to], send_all.at[a], s_sidx.at[t], r_sidx.at[a], at_px(to))
        return 0

    def start_ridx(t, _):
        to = (b + t) % PY
        send(recv_idx.at[to], recv_all.at[b], s_ridx.at[t], r_ridx.at[b], (a, to))
        return 0

    lax.fori_loop(1, PX, start_sidx, 0)
    lax.fori_loop(1, SIDE, start_stale, 0)
    lax.fori_loop(1, PY, start_ridx, 0)

    for dy in (3, 2, 1, 0):
        from_y = (y + SIDE - dy) % SIDE
        to_y = (y + dy) % SIDE

        def start_out(t, _):
            to = (a + t) % PX
            send(adj_out.at[to, from_y], a_out.at[a, from_y], s_out.at[t, dy], r_out.at[a, from_y], at_px(to))
            return 0

        def start_in(dz, _):
            to_z = (z + dz) % SIDE
            send(adj_in.at[:, to_y, to_z], a_in.at[y, z], s_in.at[dy, dz], r_in.at[y, z], at_py(to_y, to_z))
            return 0

        lax.fori_loop(1, PX, start_out, 0)
        lax.fori_loop(0 if dy else 1, SIDE, start_in, 0)
        keep(adj_out.at[a, from_y], a_out.at[a, from_y], r_out.at[a, from_y])
    keep(adj_in.at[:, y, z], a_in.at[y, z], r_in.at[y, z])

    def wait_sidx(i, _):
        wait(send_all.at[i], r_sidx.at[i])
        return 0

    def wait_ridx(j, _):
        wait(recv_all.at[j], r_ridx.at[j])
        return 0

    lax.fori_loop(0, PX, wait_sidx, 0)
    lax.fori_loop(0, PY, wait_ridx, 0)

    def gather(i):
        def body(py, _):
            index = send_all[i, py]
            hot = jnp.concatenate([hot_rows(index[k : k + 1]) for k in range(SIDE)], axis=0)
            rows = dot(hot, stale_all[i]).astype(BF16)
            for k in range(SIDE):
                rows_buf[py, k, i] = rows[k * SLOT : (k + 1) * SLOT]
            return 0

        lax.fori_loop(0, SIDE, body, 0)

    def near(d, _):
        i = (x + d) % SIDE * CORES + c
        wait(stale_all.at[i], r_stale.at[i])
        send(stale_all.at[i], stale_all.at[i], s_fwd.at[d], r_stale.at[i], at_px(x * CORES + other))
        gather(i)
        return 0

    def far(d, _):
        i = (x + d) % SIDE * CORES + other
        wait(stale_all.at[i], r_stale.at[i])
        gather(i)
        return 0

    lax.fori_loop(0, SIDE, near, 0)
    lax.fori_loop(0, SIDE, far, 0)

    total[...] = dot(local_adj[...], feats[...])

    def forward(py, pz):
        wait(a_in.at[py, pz], r_in.at[py, pz])
        p_b = py * SIDE + pz
        p = a * PY + p_b
        index = recv_all[p_b]
        same = p_b == b
        for i in range(PX):
            mine = jnp.full((SLOT, SLOT), owner[p, i * PY + b], jnp.int32) == 1
            block = jnp.where(mine, a_in[py, pz, i].astype(F32), a_out[i, py, pz].astype(F32))
            drop = jnp.full((SLOT, SLOT), jnp.where(same & (a == i), 1, 0), jnp.int32) == 1
            block = jnp.where(drop, 0.0, block).astype(BF16)
            a_in[py, pz, i] = block
            sums_buf[pl.ds(i * SLOT, SLOT)] = dot(block, rows_buf[py, pz, i]).astype(BF16)
        for r in range(2):
            hot = jnp.concatenate(
                [hot_columns(index[i : i + 1], r * FEAT, FEAT) for i in range(PX)], axis=1
            )
            part = dot(hot, sums_buf[...]).astype(BF16)
            part_z[py, pz, pl.ds(r * FEAT, FEAT)] = part[:, :HALF]
            part_y[py, pz, pl.ds(r * FEAT, FEAT)] = part[:, HALF:]

    def second_z(py):
        def arrive(d, _):
            f = (z + d) % SIDE
            wait(recv_z.at[py, f], r_z.at[py, f])
            return 0

        lax.fori_loop(1, SIDE, arrive, 0)
        acc = part_z[py, z].astype(F32)
        for d in range(1, SIDE):
            acc = acc + recv_z[py, (z + d) % SIDE].astype(F32)
        return acc

    def second_y(pz):
        acc = part_y[y, pz].astype(F32)
        for d in range(1, SIDE):
            acc = acc + recv_y[(y + d) % SIDE, pz].astype(F32)
        return acc

    for dy in (3, 2, 1, 0):
        py = (y + SIDE - dy) % SIDE

        def wait_out(i, _):
            wait(a_out.at[i, py], r_out.at[i, py])
            return 0

        lax.fori_loop(0, PX, wait_out, 0)

        def step(dz, _):
            forward(py, (z + SIDE - dz) % SIDE)
            return 0

        lax.fori_loop(0, SIDE, step, 0)

        def start_z(dz, _):
            to_z = (z + dz) % SIDE
            send(part_z.at[py, to_z], recv_z.at[py, z], s_z.at[dy, dz], r_z.at[py, z], at_py(y, to_z))
            return 0

        lax.fori_loop(1, SIDE, start_z, 0)
        if dy:
            send(part_y.at[py], recv_y.at[y], s_y.at[dy], r_y.at[y], at_py(py, z))
        if dy < SIDE - 1:
            back = (y + SIDE - dy - 1) % SIDE
            send_z2[back] = second_z(back).astype(BF16)
            send(send_z2.at[back], recv_z2.at[y], s_z2.at[dy + 1], r_z2.at[y], at_py(back, z))

    def wait_y(d, _):
        f = (y + d) % SIDE
        wait(recv_y.at[f], r_y.at[f])
        return 0

    lax.fori_loop(1, SIDE, wait_y, 0)

    def start_y2(dz, _):
        to_z = (z + dz) % SIDE
        send_y2[to_z] = second_y(to_z).astype(BF16)
        send(send_y2.at[to_z], recv_y2.at[z], s_y2.at[dz], r_y2.at[z], at_py(y, to_z))
        return 0

    lax.fori_loop(1, SIDE, start_y2, 0)
    total_y = second_y(z)
    total_z = second_z(y)
    for d in range(1, SIDE):
        f = (y + d) % SIDE
        wait(recv_z2.at[f], r_z2.at[f])
        total_z = total_z + recv_z2[f].astype(F32)
    total[:, :HALF] = total[:, :HALF] + total_z
    for d in range(1, SIDE):
        f = (z + d) % SIDE
        wait(recv_y2.at[f], r_y2.at[f])
        total_y = total_y + recv_y2[f].astype(F32)
    total[:, HALF:] = total[:, HALF:] + total_y

    summed = total[...].astype(BF16)
    pre = dot(summed, weight[...])
    pre_grad = gelu_grad(pre, cotangent[...].astype(F32)).astype(BF16)
    grad = dot(pre_grad, weight[...], 1, 1).astype(BF16)
    g_z[y, z] = grad[:, :HALF]
    g_y[y, z] = grad[:, HALF:]

    def start_g(py, pz, z_half, y_half, slot):
        if z_half:
            def along_y(d, _):
                send(g_z.at[py, pz], g_z.at[py, pz], s_gz.at[slot, d], r_gz.at[py, pz], at_py((y + d) % SIDE, z))
                return 0

            lax.fori_loop(1, SIDE, along_y, 0)
        if y_half:
            def along_z(d, _):
                send(g_y.at[py, pz], g_y.at[py, pz], s_gy.at[slot, d], r_gy.at[py, pz], at_py(y, (z + d) % SIDE))
                return 0

            lax.fori_loop(1, SIDE, along_z, 0)

    def first_g(d, _):
        send(g_z.at[y, z], g_z.at[y, z], s_gz.at[SIDE, d], r_gz.at[y, z], at_py(y, (z + d) % SIDE))
        send(g_y.at[y, z], g_y.at[y, z], s_gy.at[SIDE, d], r_gy.at[y, z], at_py((y + d) % SIDE, z))
        return 0

    lax.fori_loop(1, SIDE, first_g, 0)
    start_g(y, z, True, True, 0)

    w_term[...] = dot(summed, pre_grad, 0, 0).reshape(PY, PART, FEAT)

    def start_w(t, _):
        to = (b + t) % PY
        send(w_term.at[to], w_parts.at[b], s_w.at[t], r_w.at[b], (a, to))
        return 0

    lax.fori_loop(1, PY, start_w, 0)
    out_feats[...] = jax.nn.gelu(pre).astype(BF16)
    feat_grad[...] = dot(local_adj[...], grad, 0, 0).astype(BF16)

    def backward(py, pz):
        index = recv_all[py * SIDE + pz]
        grad_p = jnp.concatenate([g_z[py, pz], g_y[py, pz]], axis=1)
        for h in range(2):
            hot = jnp.concatenate([hot_rows(index[i : i + 1]) for i in range(h * 4, h * 4 + 4)], axis=0)
            rows = dot(hot, grad_p).astype(BF16)
            for k in range(4):
                i = h * 4 + k
                rows_buf[py, pz, i] = dot(
                    a_in[py, pz, i], rows[k * SLOT : (k + 1) * SLOT], 0, 0
                ).astype(BF16)

    backward(y, z)

    def pass_on(d, _):
        f_z, f_y = (z + d) % SIDE, (y + d) % SIDE
        wait(g_z.at[y, f_z], r_gz.at[y, f_z])
        start_g(y, f_z, True, False, d)
        wait(g_y.at[f_y, z], r_gy.at[f_y, z])
        start_g(f_y, z, False, True, d)
        return 0

    def along_z(d, _):
        f = (z + d) % SIDE
        wait(g_y.at[y, f], r_gy.at[y, f])
        backward(y, f)
        return 0

    def along_y(d, _):
        f = (y + d) % SIDE
        wait(g_z.at[f, z], r_gz.at[f, z])
        backward(f, z)
        return 0

    lax.fori_loop(1, SIDE, pass_on, 0)
    lax.fori_loop(1, SIDE, along_z, 0)
    lax.fori_loop(1, SIDE, along_y, 0)

    w_sum[a] = w_term[b]

    def add_w(t, _):
        f = (b + t) % PY
        wait(w_parts.at[f], r_w.at[f])
        w_sum[a] = w_sum[a] + w_parts[f]
        return 0

    lax.fori_loop(1, PY, add_w, 0)

    def start_w2(t, _):
        send(w_sum.at[a], w_parts2.at[a], s_w2.at[t], r_w2.at[a], at_px((a + t) % PX))
        return 0

    lax.fori_loop(1, PX, start_w2, 0)

    def diagonal(t, _):
        py = (y + t // 3 + 1) % SIDE
        pz = (z + t % 3 + 1) % SIDE
        wait(g_z.at[py, pz], r_gz.at[py, pz])
        wait(g_y.at[py, pz], r_gy.at[py, pz])
        backward(py, pz)
        return 0

    lax.fori_loop(0, 5, diagonal, 0)

    w_parts2[a] = w_sum[a]

    def wait_w2(t, _):
        f = (a + t) % PX
        wait(w_parts2.at[f], r_w2.at[f])
        return 0

    lax.fori_loop(1, PX, wait_w2, 0)
    acc = w_parts2[0]
    for i in range(1, PX):
        acc = acc + w_parts2[i]
    w_all[b] = acc * F32(1.0 / (PX * PY * ROWS) ** 0.5)

    def start_w3(t, _):
        to = (b + t) % PY
        send(w_all.at[b], w_all.at[b], s_w3.at[t], r_w3.at[b], (a, to))
        return 0

    lax.fori_loop(1, PY, start_w3, 0)
    lax.fori_loop(5, 9, diagonal, 0)

    def scatter(i):
        acc = jnp.zeros((ROWS, FEAT), F32)
        for py in range(SIDE):
            index = send_all[i, py]
            hot = jnp.concatenate([hot_columns(index[k : k + 1], 0, ROWS) for k in range(SIDE)], axis=1)
            rows = jnp.concatenate([rows_buf[py, k, i] for k in range(SIDE)], axis=0)
            acc = acc + dot(hot, rows)
        return acc

    def start_core(d, _):
        to_x = (x + d) % SIDE
        bound_core[to_x] = scatter(to_x * CORES + other).astype(BF16)
        send(bound_core.at[to_x], recv_core.at[to_x], s_core.at[d], r_core.at[to_x], at_px(x * CORES + other))
        return 0

    lax.fori_loop(0, SIDE, start_core, 0)

    def start_x(d, _):
        to_x = (x + d) % SIDE
        acc = scatter(to_x * CORES + c)
        wait(recv_core.at[to_x], r_core.at[to_x])
        bound_x[to_x] = (acc + recv_core[to_x].astype(F32)).astype(BF16)
        send(bound_x.at[to_x], recv_x.at[x], s_x.at[d], r_x.at[x], at_px(to_x * CORES + c))
        return 0

    lax.fori_loop(1, SIDE, start_x, 0)
    acc = scatter(a)
    wait(recv_core.at[x], r_core.at[x])
    acc = acc + recv_core[x].astype(F32)

    def wait_w3(t, _):
        f = (b + t) % PY
        wait(w_all.at[f], r_w3.at[f])
        return 0

    lax.fori_loop(1, PY, wait_w3, 0)
    weight_grad[...] = w_all[...].reshape(FEAT, FEAT)

    for d in range(1, SIDE):
        f = (x + d) % SIDE
        wait(recv_x.at[f], r_x.at[f])
        acc = acc + recv_x[f].astype(F32)
    bound_grad[...] = acc.astype(BF16)

    def done_px(t, _):
        wait(send_all.at[0], s_sidx.at[t])
        for dy in range(SIDE):
            wait(a_out.at[0, 0], s_out.at[t, dy])
        wait(w_sum.at[0], s_w2.at[t])
        return 0

    def done_py(t, _):
        wait(recv_all.at[0], s_ridx.at[t])
        wait(w_term.at[0], s_w.at[t])
        wait(w_all.at[0], s_w3.at[t])
        return 0

    def done_in(t, _):
        wait(a_in.at[0, 0], s_in.at[t // SIDE, t % SIDE])
        return 0

    def done_side(d, _):
        wait(stale_all.at[0], s_stale.at[d])
        for dy in range(SIDE):
            wait(part_z.at[0, 0], s_z.at[dy, d])
        wait(part_y.at[0], s_y.at[d])
        wait(send_z2.at[0], s_z2.at[d])
        wait(send_y2.at[0], s_y2.at[d])
        for k in range(SIDE + 1):
            wait(g_z.at[0, 0], s_gz.at[k, d])
            wait(g_y.at[0, 0], s_gy.at[k, d])
        wait(bound_x.at[0], s_x.at[d])
        return 0

    def done_core(d, _):
        wait(stale_all.at[0], s_fwd.at[d])
        wait(bound_core.at[0], s_core.at[d])
        return 0

    lax.fori_loop(1, PX, done_px, 0)
    lax.fori_loop(1, PY, done_py, 0)
    lax.fori_loop(1, PY, done_in, 0)
    lax.fori_loop(1, SIDE, done_side, 0)
    lax.fori_loop(0, SIDE, done_core, 0)


def on_device(
    feats, stale_feats, local_adj, adj_in, adj_out, owner, send_idx, recv_idx, weight, cotangent
):
    hbm = pl.BlockSpec(memory_space=pl.ANY)
    vmem = pl.BlockSpec(memory_space=pltpu.VMEM)
    dma = lambda *shape: pltpu.SemaphoreType.DMA(shape)
    node = lambda *shape: pltpu.VMEM((*shape, ROWS, HALF), BF16)
    return pl.pallas_call(
        kernel,
        out_shape=(
            jax.ShapeDtypeStruct((ROWS, FEAT), BF16),
            jax.ShapeDtypeStruct((ROWS, FEAT), BF16),
            jax.ShapeDtypeStruct((ROWS, FEAT), BF16),
            jax.ShapeDtypeStruct((FEAT, FEAT), F32),
        ),
        in_specs=[hbm] * 5 + [pl.BlockSpec(memory_space=pltpu.SMEM)] + [vmem] * 4,
        out_specs=(vmem,) * 4,
        scratch_shapes=[
            pltpu.VMEM((SIDE, SIDE, PX, SLOT, SLOT), BF16),
            pltpu.VMEM((PX, SIDE, SIDE, SLOT, SLOT), BF16),
            pltpu.VMEM((PX, ROWS, FEAT), BF16),
            pltpu.VMEM((PX, SIDE, SIDE, SLOT), jnp.int32),
            pltpu.VMEM((PY, PX, SLOT), jnp.int32),
            pltpu.VMEM((SIDE, SIDE, PX, SLOT, FEAT), BF16),
            pltpu.VMEM((PX * SLOT, FEAT), BF16),
            node(SIDE, SIDE),
            node(SIDE, SIDE),
            node(SIDE, SIDE),
            node(SIDE, SIDE),
            node(SIDE),
            node(SIDE),
            node(SIDE),
            node(SIDE),
            pltpu.VMEM((ROWS, FEAT), F32),
            node(SIDE, SIDE),
            node(SIDE, SIDE),
            pltpu.VMEM((SIDE, ROWS, FEAT), BF16),
            pltpu.VMEM((SIDE, ROWS, FEAT), BF16),
            pltpu.VMEM((SIDE, ROWS, FEAT), BF16),
            pltpu.VMEM((SIDE, ROWS, FEAT), BF16),
            pltpu.VMEM((PY, PART, FEAT), F32),
            pltpu.VMEM((PY, PART, FEAT), F32),
            pltpu.VMEM((PX, PART, FEAT), F32),
            pltpu.VMEM((PX, PART, FEAT), F32),
            pltpu.VMEM((PY, PART, FEAT), F32),
            dma(PY), dma(PY), dma(PX), dma(PX),
            dma(SIDE), dma(PX), dma(SIDE),
            dma(PX, SIDE), dma(PX, SIDE), dma(SIDE, SIDE), dma(SIDE, SIDE),
            dma(SIDE, SIDE), dma(SIDE, SIDE), dma(SIDE), dma(SIDE),
            dma(SIDE), dma(SIDE), dma(SIDE), dma(SIDE),
            dma(SIDE + 1, SIDE), dma(SIDE, SIDE), dma(SIDE + 1, SIDE), dma(SIDE, SIDE),
            dma(SIDE), dma(SIDE), dma(SIDE), dma(SIDE),
            dma(PY), dma(PY), dma(PX), dma(PX), dma(PY), dma(PY),
        ],
        compiler_params=pltpu.CompilerParams(
            collective_id=0, has_side_effects=True, vmem_limit_bytes=60 * 2**20
        ),
    )(
        adj_in.reshape(PX, SIDE, SIDE, SLOT, SLOT),
        adj_out.reshape(PX, SIDE, SIDE, SLOT, SLOT),
        stale_feats,
        send_idx.reshape(PX, SIDE, SIDE, SLOT),
        recv_idx.reshape(PX, PY, SLOT).transpose(1, 0, 2),
        owner,
        feats,
        local_adj,
        weight,
        cotangent,
    )


def solution(mesh):
    both = ("px", "py")
    in_specs = (
        P(both, None),
        P(both, None),
        P(both, None),
        P(both, None, None),
        P(both, None, None),
        P(),
        P(both, None),
        P(both, None),
        P(),
        P(both, None),
    )
    out_specs = (P(both, None), P(both, None), P(both, None), P())
    return jax.shard_map(
        on_device, mesh=mesh, in_specs=in_specs, out_specs=out_specs, check_vma=False
    )
```

```python
import functools

import jax
import jax.numpy as jnp
from jax import lax
from jax.experimental import pallas as pl
from jax.experimental.pallas import tpu as pltpu
from jax.sharding import PartitionSpec as P

F32 = jnp.float32
BF16 = jnp.bfloat16
MESH = pl.DeviceIdType.MESH
PX, PY, CORES, SIDE = 8, 16, 2, 4
SLOT, ROWS, FEAT = 128, 512, 256
HALF = FEAT // 2
PART = FEAT // PY
GROUPS = (2, 1, 3, 0)


def gelu_grad(pre, grad):
    return jax.vjp(jax.nn.gelu, pre)[1](grad)[0]


def dot(left, right, left_dim=1, right_dim=0):
    return lax.dot_general(
        left, right, (((left_dim,), (right_dim,)), ((), ())), preferred_element_type=F32
    )


def hot_rows(index):
    column = jnp.broadcast_to(index.astype(F32), (SLOT, SLOT)).T
    lane = lax.broadcasted_iota(jnp.int32, (SLOT, SLOT), 1).astype(F32)
    return jnp.concatenate(
        [jnp.where(column == lane + F32(t * SLOT), 1.0, 0.0).astype(BF16) for t in range(ROWS // SLOT)],
        axis=1,
    )


def hot_columns(index, first, count):
    row = lax.broadcasted_iota(jnp.int32, (count, SLOT), 0) + first
    return jnp.where(row == index, 1.0, 0.0).astype(BF16)


def kernel(
    adj_in, adj_out, stale, send_idx, recv_idx, owner, feats, local_adj, weight, cotangent,
    out_feats, feat_grad, bound_grad, weight_grad,
    a_in, a_out, stale_all, send_all, recv_all, rows_buf, sums_buf, part_z, part_y, recv_z, recv_y,
    send_z2, send_y2, recv_z2, recv_y2, total, g_z, g_y, bound_core, bound_x, recv_core, recv_x,
    w_term, w_parts, w_sum, w_parts2, w_all,
    s_ridx, r_ridx, s_sidx, r_sidx, s_stale, r_stale, s_fwd, s_out, r_out, s_in, r_in,
    s_z, r_z, s_y, r_y, s_z2, r_z2, s_y2, r_y2,
    s_gz, r_gz, s_gy, r_gy, s_core, r_core, s_x, r_x, s_w, r_w, s_w2, r_w2, s_w3, r_w3,
):
    a, b = lax.axis_index("px"), lax.axis_index("py")
    x, c = a // CORES, a % CORES
    y, z = b // SIDE, b % SIDE
    other = 1 - c

    def at_px(to):
        return (to, b)

    def at_py(to_y, to_z):
        return (a, to_y * SIDE + to_z)

    def send(src, dst, s_sem, r_sem, to):
        pltpu.make_async_remote_copy(
            src_ref=src, dst_ref=dst, send_sem=s_sem, recv_sem=r_sem, device_id=to, device_id_type=MESH
        ).start()

    def keep(src, dst, sem):
        pltpu.make_async_copy(src, dst, sem).start()

    def wait(ref, sem):
        pltpu.make_async_copy(ref, ref, sem).wait()

    barrier = pltpu.get_barrier_semaphore()

    def greet_px(t, _):
        pl.semaphore_signal(barrier, inc=1, device_id=at_px((a + t) % PX), device_id_type=MESH)
        return 0

    def greet_py(t, _):
        to = (b + t) % PY
        pl.semaphore_signal(barrier, inc=1, device_id=(a, to), device_id_type=MESH)
        return 0

    lax.fori_loop(1, PX, greet_px, 0)
    lax.fori_loop(1, PY, greet_py, 0)
    pl.semaphore_wait(barrier, PX - 1 + PY - 1)

    keep(stale, stale_all.at[a], r_stale.at[a])
    keep(send_idx.at[a], send_all.at[a], r_sidx.at[a])
    keep(recv_idx.at[:, b], recv_all.at[b], r_ridx.at[b])

    def start_stale(d, _):
        send(stale, stale_all.at[a], s_stale.at[d], r_stale.at[a], at_px((x + d) % SIDE * CORES + c))
        return 0

    def start_sidx(t, _):
        to = (a + t) % PX
        send(send_idx.at[to], send_all.at[a], s_sidx.at[t], r_sidx.at[a], at_px(to))
        return 0

    def start_ridx(t, _):
        to = (b + t) % PY
        send(recv_idx.at[:, to], recv_all.at[b], s_ridx.at[t], r_ridx.at[b], (a, to))
        return 0

    lax.fori_loop(1, PX, start_sidx, 0)
    lax.fori_loop(1, SIDE, start_stale, 0)
    lax.fori_loop(1, PY, start_ridx, 0)

    for k in GROUPS:
        def start_group(dy, _):
            dz = (dy + k) % SIDE
            to_y, to_z = (y + dy) % SIDE, (z + dz) % SIDE
            from_y, from_z = (y + SIDE - dy) % SIDE, (z + SIDE - dz) % SIDE

            @pl.when(dy + dz > 0)
            def _():
                send(adj_in.at[:, to_y, to_z], a_in.at[y, z], s_in.at[dy, dz], r_in.at[y, z], at_py(to_y, to_z))

            def start_out(t, _):
                to = (a + t) % PX
                send(
                    adj_out.at[to, from_y, from_z], a_out.at[a, from_y, from_z],
                    s_out.at[t, k], r_out.at[a, k], at_px(to),
                )
                return 0

            lax.fori_loop(1, PX, start_out, 0)
            keep(adj_out.at[a, from_y, from_z], a_out.at[a, from_y, from_z], r_out.at[a, k])
            return 0

        lax.fori_loop(0, SIDE, start_group, 0)
    keep(adj_in.at[:, y, z], a_in.at[y, z], r_in.at[y, z])

    def wait_sidx(i, _):
        wait(send_all.at[i], r_sidx.at[i])
        return 0

    def wait_ridx(j, _):
        wait(recv_all.at[j], r_ridx.at[j])
        return 0

    lax.fori_loop(0, PX, wait_sidx, 0)
    lax.fori_loop(0, PY, wait_ridx, 0)

    def gather(i):
        def body(py, _):
            index = send_all[i, py]
            hot = jnp.concatenate([hot_rows(index[k : k + 1]) for k in range(SIDE)], axis=0)
            rows = dot(hot, stale_all[i]).astype(BF16)
            for k in range(SIDE):
                rows_buf[py, k, i] = rows[k * SLOT : (k + 1) * SLOT]
            return 0

        lax.fori_loop(0, SIDE, body, 0)

    def near(d, _):
        i = (x + d) % SIDE * CORES + c
        wait(stale_all.at[i], r_stale.at[i])
        send(stale_all.at[i], stale_all.at[i], s_fwd.at[d], r_stale.at[i], at_px(x * CORES + other))
        gather(i)
        return 0

    def far(d, _):
        i = (x + d) % SIDE * CORES + other
        wait(stale_all.at[i], r_stale.at[i])
        gather(i)
        return 0

    lax.fori_loop(0, SIDE, near, 0)
    lax.fori_loop(0, SIDE, far, 0)

    total[...] = dot(local_adj[...], feats[...])

    def forward(py, pz):
        wait(a_in.at[py, pz], r_in.at[py, pz])
        p_b = py * SIDE + pz
        p = a * PY + p_b
        index = recv_all[p_b]
        same = p_b == b
        for i in range(PX):
            mine = jnp.full((SLOT, SLOT), owner[p, i * PY + b], jnp.int32) == 1
            block = jnp.where(mine, a_in[py, pz, i].astype(F32), a_out[i, py, pz].astype(F32))
            drop = jnp.full((SLOT, SLOT), jnp.where(same & (a == i), 1, 0), jnp.int32) == 1
            block = jnp.where(drop, 0.0, block).astype(BF16)
            a_in[py, pz, i] = block
            sums_buf[pl.ds(i * SLOT, SLOT)] = dot(block, rows_buf[py, pz, i]).astype(BF16)
        for r in range(2):
            hot = jnp.concatenate(
                [hot_columns(index[i : i + 1], r * FEAT, FEAT) for i in range(PX)], axis=1
            )
            part = dot(hot, sums_buf[...]).astype(BF16)
            part_z[py, pz, pl.ds(r * FEAT, FEAT)] = part[:, :HALF]
            part_y[py, pz, pl.ds(r * FEAT, FEAT)] = part[:, HALF:]

    def second_z(py):
        def arrive(d, _):
            f = (z + d) % SIDE
            wait(recv_z.at[py, f], r_z.at[py, f])
            return 0

        lax.fori_loop(1, SIDE, arrive, 0)
        acc = part_z[py, z].astype(F32)
        for d in range(1, SIDE):
            acc = acc + recv_z[py, (z + d) % SIDE].astype(F32)
        return acc

    def second_y(pz):
        def arrive(d, _):
            f = (y + d) % SIDE
            wait(recv_y.at[f, pz], r_y.at[f, pz])
            return 0

        lax.fori_loop(1, SIDE, arrive, 0)
        acc = part_y[y, pz].astype(F32)
        for d in range(1, SIDE):
            acc = acc + recv_y[(y + d) % SIDE, pz].astype(F32)
        return acc

    for k in GROUPS:

        def wait_out(i, _):
            wait(a_out.at[i, 0], r_out.at[i, k])
            return 0

        lax.fori_loop(0, PX, wait_out, 0)

        def step(dy, _):
            dz = (dy + k) % SIDE
            py, pz = (y + SIDE - dy) % SIDE, (z + SIDE - dz) % SIDE
            forward(py, pz)

            @pl.when(dz > 0)
            def _():
                send(part_z.at[py, pz], recv_z.at[py, z], s_z.at[dy, dz], r_z.at[py, z], at_py(y, pz))

            @pl.when(dy > 0)
            def _():
                send(part_y.at[py, pz], recv_y.at[y, pz], s_y.at[dy, dz], r_y.at[y, pz], at_py(py, z))

            return 0

        lax.fori_loop(0, SIDE, step, 0)

    def start_second(d, _):
        to_y, to_z = (y + d) % SIDE, (z + d) % SIDE
        send_z2[to_y] = second_z(to_y).astype(BF16)
        send(send_z2.at[to_y], recv_z2.at[y], s_z2.at[d], r_z2.at[y], at_py(to_y, z))
        send_y2[to_z] = second_y(to_z).astype(BF16)
        send(send_y2.at[to_z], recv_y2.at[z], s_y2.at[d], r_y2.at[z], at_py(y, to_z))
        return 0

    lax.fori_loop(1, SIDE, start_second, 0)
    total_y = second_y(z)
    total_z = second_z(y)
    for d in range(1, SIDE):
        f = (y + d) % SIDE
        wait(recv_z2.at[f], r_z2.at[f])
        total_z = total_z + recv_z2[f].astype(F32)
    total[:, :HALF] = total[:, :HALF] + total_z
    for d in range(1, SIDE):
        f = (z + d) % SIDE
        wait(recv_y2.at[f], r_y2.at[f])
        total_y = total_y + recv_y2[f].astype(F32)
    total[:, HALF:] = total[:, HALF:] + total_y

    summed = total[...].astype(BF16)
    pre = dot(summed, weight[...])
    pre_grad = gelu_grad(pre, cotangent[...].astype(F32)).astype(BF16)
    grad = dot(pre_grad, weight[...], 1, 1).astype(BF16)
    g_z[y, z] = grad[:, :HALF]
    g_y[y, z] = grad[:, HALF:]

    def start_g(py, pz, z_half, y_half, slot):
        if z_half:
            def along_y(d, _):
                send(g_z.at[py, pz], g_z.at[py, pz], s_gz.at[slot, d], r_gz.at[py, pz], at_py((y + d) % SIDE, z))
                return 0

            lax.fori_loop(1, SIDE, along_y, 0)
        if y_half:
            def along_z(d, _):
                send(g_y.at[py, pz], g_y.at[py, pz], s_gy.at[slot, d], r_gy.at[py, pz], at_py(y, (z + d) % SIDE))
                return 0

            lax.fori_loop(1, SIDE, along_z, 0)

    def first_g(d, _):
        send(g_z.at[y, z], g_z.at[y, z], s_gz.at[SIDE, d], r_gz.at[y, z], at_py(y, (z + d) % SIDE))
        send(g_y.at[y, z], g_y.at[y, z], s_gy.at[SIDE, d], r_gy.at[y, z], at_py((y + d) % SIDE, z))
        return 0

    lax.fori_loop(1, SIDE, first_g, 0)
    start_g(y, z, True, True, 0)

    w_term[...] = dot(summed, pre_grad, 0, 0).reshape(PY, PART, FEAT)

    def start_w(t, _):
        to = (b + t) % PY
        send(w_term.at[to], w_parts.at[b], s_w.at[t], r_w.at[b], (a, to))
        return 0

    lax.fori_loop(1, PY, start_w, 0)
    out_feats[...] = jax.nn.gelu(pre).astype(BF16)
    feat_grad[...] = dot(local_adj[...], grad, 0, 0).astype(BF16)

    def backward(py, pz):
        index = recv_all[py * SIDE + pz]
        grad_p = jnp.concatenate([g_z[py, pz], g_y[py, pz]], axis=1)
        for h in range(2):
            hot = jnp.concatenate([hot_rows(index[i : i + 1]) for i in range(h * 4, h * 4 + 4)], axis=0)
            rows = dot(hot, grad_p).astype(BF16)
            for k in range(4):
                i = h * 4 + k
                rows_buf[py, pz, i] = dot(
                    a_in[py, pz, i], rows[k * SLOT : (k + 1) * SLOT], 0, 0
                ).astype(BF16)

    backward(y, z)

    def pass_on(d, _):
        f_z, f_y = (z + d) % SIDE, (y + d) % SIDE
        wait(g_z.at[y, f_z], r_gz.at[y, f_z])
        start_g(y, f_z, True, False, d)
        wait(g_y.at[f_y, z], r_gy.at[f_y, z])
        start_g(f_y, z, False, True, d)
        return 0

    def along_z(d, _):
        f = (z + d) % SIDE
        wait(g_y.at[y, f], r_gy.at[y, f])
        backward(y, f)
        return 0

    def along_y(d, _):
        f = (y + d) % SIDE
        wait(g_z.at[f, z], r_gz.at[f, z])
        backward(f, z)
        return 0

    lax.fori_loop(1, SIDE, pass_on, 0)
    lax.fori_loop(1, SIDE, along_z, 0)
    lax.fori_loop(1, SIDE, along_y, 0)

    w_sum[a] = w_term[b]

    def add_w(t, _):
        f = (b + t) % PY
        wait(w_parts.at[f], r_w.at[f])
        w_sum[a] = w_sum[a] + w_parts[f]
        return 0

    lax.fori_loop(1, PY, add_w, 0)

    def start_w2(t, _):
        send(w_sum.at[a], w_parts2.at[a], s_w2.at[t], r_w2.at[a], at_px((a + t) % PX))
        return 0

    lax.fori_loop(1, PX, start_w2, 0)

    def diagonal(t, _):
        py = (y + t // 3 + 1) % SIDE
        pz = (z + t % 3 + 1) % SIDE
        wait(g_z.at[py, pz], r_gz.at[py, pz])
        wait(g_y.at[py, pz], r_gy.at[py, pz])
        backward(py, pz)
        return 0

    lax.fori_loop(0, 5, diagonal, 0)

    w_parts2[a] = w_sum[a]

    def wait_w2(t, _):
        f = (a + t) % PX
        wait(w_parts2.at[f], r_w2.at[f])
        return 0

    lax.fori_loop(1, PX, wait_w2, 0)
    acc = w_parts2[0]
    for i in range(1, PX):
        acc = acc + w_parts2[i]
    w_all[b] = acc * F32(1.0 / (PX * PY * ROWS) ** 0.5)

    def start_w3(t, _):
        to = (b + t) % PY
        send(w_all.at[b], w_all.at[b], s_w3.at[t], r_w3.at[b], (a, to))
        return 0

    lax.fori_loop(1, PY, start_w3, 0)
    lax.fori_loop(5, 9, diagonal, 0)

    def scatter(i):
        acc = jnp.zeros((ROWS, FEAT), F32)
        for py in range(SIDE):
            index = send_all[i, py]
            hot = jnp.concatenate([hot_columns(index[k : k + 1], 0, ROWS) for k in range(SIDE)], axis=1)
            rows = jnp.concatenate([rows_buf[py, k, i] for k in range(SIDE)], axis=0)
            acc = acc + dot(hot, rows)
        return acc

    def start_core(d, _):
        to_x = (x + d) % SIDE
        bound_core[to_x] = scatter(to_x * CORES + other).astype(BF16)
        send(bound_core.at[to_x], recv_core.at[to_x], s_core.at[d], r_core.at[to_x], at_px(x * CORES + other))
        return 0

    lax.fori_loop(0, SIDE, start_core, 0)

    def start_x(d, _):
        to_x = (x + d) % SIDE
        acc = scatter(to_x * CORES + c)
        wait(recv_core.at[to_x], r_core.at[to_x])
        bound_x[to_x] = (acc + recv_core[to_x].astype(F32)).astype(BF16)
        send(bound_x.at[to_x], recv_x.at[x], s_x.at[d], r_x.at[x], at_px(to_x * CORES + c))
        return 0

    lax.fori_loop(1, SIDE, start_x, 0)
    acc = scatter(a)
    wait(recv_core.at[x], r_core.at[x])
    acc = acc + recv_core[x].astype(F32)

    def wait_w3(t, _):
        f = (b + t) % PY
        wait(w_all.at[f], r_w3.at[f])
        return 0

    lax.fori_loop(1, PY, wait_w3, 0)
    weight_grad[...] = w_all[...].reshape(FEAT, FEAT)

    for d in range(1, SIDE):
        f = (x + d) % SIDE
        wait(recv_x.at[f], r_x.at[f])
        acc = acc + recv_x[f].astype(F32)
    bound_grad[...] = acc.astype(BF16)

    def done_px(t, _):
        wait(send_all.at[0], s_sidx.at[t])
        for k in range(SIDE):
            wait(a_out.at[0, 0], s_out.at[t, k])
        wait(w_sum.at[0], s_w2.at[t])
        return 0

    def done_py(t, _):
        wait(recv_all.at[0], s_ridx.at[t])
        wait(w_term.at[0], s_w.at[t])
        wait(w_all.at[0], s_w3.at[t])
        return 0

    def done_in(t, _):
        wait(a_in.at[0, 0], s_in.at[t // SIDE, t % SIDE])
        return 0

    def done_side(d, _):
        wait(stale_all.at[0], s_stale.at[d])
        for k in range(SIDE):
            wait(part_z.at[0, 0], s_z.at[k, d])
            wait(part_y.at[0, 0], s_y.at[d, k])
        wait(send_z2.at[0], s_z2.at[d])
        wait(send_y2.at[0], s_y2.at[d])
        for k in range(SIDE + 1):
            wait(g_z.at[0, 0], s_gz.at[k, d])
            wait(g_y.at[0, 0], s_gy.at[k, d])
        wait(bound_x.at[0], s_x.at[d])
        return 0

    def done_core(d, _):
        wait(stale_all.at[0], s_fwd.at[d])
        wait(bound_core.at[0], s_core.at[d])
        return 0

    lax.fori_loop(1, PX, done_px, 0)
    lax.fori_loop(1, PY, done_py, 0)
    lax.fori_loop(1, PY, done_in, 0)
    lax.fori_loop(1, SIDE, done_side, 0)
    lax.fori_loop(0, SIDE, done_core, 0)


def hand_over(*refs):
    count = len(refs) // 2
    for source, result in zip(refs[:count], refs[count:]):
        result[...] = source[...]


def on_device(
    feats, stale_feats, local_adj, adj_in, adj_out, owner, send_idx, recv_idx, weight, cotangent
):
    hbm = pl.BlockSpec(memory_space=pl.ANY)
    vmem = pl.BlockSpec(memory_space=pltpu.VMEM)
    dma = lambda *shape: pltpu.SemaphoreType.DMA(shape)
    node = lambda *shape: pltpu.VMEM((*shape, ROWS, HALF), BF16)
    shapes = (
        jax.ShapeDtypeStruct((ROWS, FEAT), BF16),
        jax.ShapeDtypeStruct((ROWS, FEAT), BF16),
        jax.ShapeDtypeStruct((ROWS, FEAT), BF16),
        jax.ShapeDtypeStruct((FEAT, FEAT), F32),
    )
    results = pl.pallas_call(
        kernel,
        out_shape=shapes,
        in_specs=[hbm] * 5 + [pl.BlockSpec(memory_space=pltpu.SMEM)] + [vmem] * 4,
        out_specs=(vmem,) * 4,
        scratch_shapes=[
            pltpu.VMEM((SIDE, SIDE, PX, SLOT, SLOT), BF16),
            pltpu.VMEM((PX, SIDE, SIDE, SLOT, SLOT), BF16),
            pltpu.VMEM((PX, ROWS, FEAT), BF16),
            pltpu.VMEM((PX, SIDE, SIDE, SLOT), jnp.int32),
            pltpu.VMEM((PY, PX, SLOT), jnp.int32),
            pltpu.VMEM((SIDE, SIDE, PX, SLOT, FEAT), BF16),
            pltpu.VMEM((PX * SLOT, FEAT), BF16),
            node(SIDE, SIDE),
            node(SIDE, SIDE),
            node(SIDE, SIDE),
            node(SIDE, SIDE),
            node(SIDE),
            node(SIDE),
            node(SIDE),
            node(SIDE),
            pltpu.VMEM((ROWS, FEAT), F32),
            node(SIDE, SIDE),
            node(SIDE, SIDE),
            pltpu.VMEM((SIDE, ROWS, FEAT), BF16),
            pltpu.VMEM((SIDE, ROWS, FEAT), BF16),
            pltpu.VMEM((SIDE, ROWS, FEAT), BF16),
            pltpu.VMEM((SIDE, ROWS, FEAT), BF16),
            pltpu.VMEM((PY, PART, FEAT), F32),
            pltpu.VMEM((PY, PART, FEAT), F32),
            pltpu.VMEM((PX, PART, FEAT), F32),
            pltpu.VMEM((PX, PART, FEAT), F32),
            pltpu.VMEM((PY, PART, FEAT), F32),
            dma(PY), dma(PY), dma(PX), dma(PX),
            dma(SIDE), dma(PX), dma(SIDE),
            dma(PX, SIDE), dma(PX, SIDE), dma(SIDE, SIDE), dma(SIDE, SIDE),
            dma(SIDE, SIDE), dma(SIDE, SIDE), dma(SIDE, SIDE), dma(SIDE, SIDE),
            dma(SIDE), dma(SIDE), dma(SIDE), dma(SIDE),
            dma(SIDE + 1, SIDE), dma(SIDE, SIDE), dma(SIDE + 1, SIDE), dma(SIDE, SIDE),
            dma(SIDE), dma(SIDE), dma(SIDE), dma(SIDE),
            dma(PY), dma(PY), dma(PX), dma(PX), dma(PY), dma(PY),
        ],
        compiler_params=pltpu.CompilerParams(
            collective_id=0, has_side_effects=True, vmem_limit_bytes=60 * 2**20
        ),
    )(
        adj_in.reshape(PX, SIDE, SIDE, SLOT, SLOT),
        adj_out.reshape(PX, SIDE, SIDE, SLOT, SLOT),
        stale_feats,
        send_idx.reshape(PX, SIDE, SIDE, SLOT),
        recv_idx.reshape(PX, PY, SLOT),
        owner,
        feats,
        local_adj,
        weight,
        cotangent,
    )
    return pl.pallas_call(
        hand_over, out_shape=shapes, in_specs=[vmem] * 4, out_specs=(vmem,) * 4
    )(*results)


def solution(mesh):
    both = ("px", "py")
    in_specs = (
        P(both, None),
        P(both, None),
        P(both, None),
        P(both, None, None),
        P(both, None, None),
        P(),
        P(both, None),
        P(both, None),
        P(),
        P(both, None),
    )
    out_specs = (P(both, None), P(both, None), P(both, None), P())
    return jax.shard_map(
        on_device, mesh=mesh, in_specs=in_specs, out_specs=out_specs, check_vma=False
    )
```

```python
import functools

import jax
import jax.numpy as jnp
from jax import lax
from jax.experimental import pallas as pl
from jax.experimental.pallas import tpu as pltpu
from jax.sharding import PartitionSpec as P

F32 = jnp.float32
BF16 = jnp.bfloat16
MESH = pl.DeviceIdType.MESH
PX, PY, CORES, SIDE = 8, 16, 2, 4
SLOT, ROWS, FEAT = 128, 512, 256
HALF = FEAT // 2
PART = FEAT // PY
GROUPS = (2, 1, 3, 0)


def gelu_grad(pre, grad):
    return jax.vjp(jax.nn.gelu, pre)[1](grad)[0]


def dot(left, right, left_dim=1, right_dim=0):
    return lax.dot_general(
        left, right, (((left_dim,), (right_dim,)), ((), ())), preferred_element_type=F32
    )


def hot_rows(index):
    column = jnp.broadcast_to(index.astype(F32), (SLOT, SLOT)).T
    lane = lax.broadcasted_iota(jnp.int32, (SLOT, SLOT), 1).astype(F32)
    return jnp.concatenate(
        [jnp.where(column == lane + F32(t * SLOT), 1.0, 0.0).astype(BF16) for t in range(ROWS // SLOT)],
        axis=1,
    )


def hot_columns(index, first, count):
    row = lax.broadcasted_iota(jnp.int32, (count, SLOT), 0) + first
    return jnp.where(row == index, 1.0, 0.0).astype(BF16)


def kernel(
    adj_in, adj_out, stale, send_idx, recv_idx, owner, feats, local_adj, weight, cotangent,
    out_feats, feat_grad, bound_grad, weight_grad,
    a_in, a_out, stale_all, send_all, recv_all, rows_buf, sums_buf, part_z, part_y, recv_z, recv_y,
    send_z2, send_y2, recv_z2, recv_y2, total, g_z, g_y, bound_core, bound_x, recv_core, recv_x,
    w_term, w_parts, w_sum, w_parts2, w_all,
    s_ridx, r_ridx, s_sidx, r_sidx, s_stale, r_stale, s_fwd, s_out, r_out, s_in, r_in,
    s_z, r_z, s_y, r_y, s_z2, r_z2, s_y2, r_y2,
    s_gz, r_gz, s_gy, r_gy, s_hz, s_hy, s_core, r_core, s_x, r_x, s_w, r_w, s_w2, r_w2, s_w3, r_w3,
):
    a, b = lax.axis_index("px"), lax.axis_index("py")
    x, c = a // CORES, a % CORES
    y, z = b // SIDE, b % SIDE
    other = 1 - c

    def at_px(to):
        return (to, b)

    def at_py(to_y, to_z):
        return (a, to_y * SIDE + to_z)

    def send(src, dst, s_sem, r_sem, to):
        pltpu.make_async_remote_copy(
            src_ref=src, dst_ref=dst, send_sem=s_sem, recv_sem=r_sem, device_id=to, device_id_type=MESH
        ).start()

    def keep(src, dst, sem):
        pltpu.make_async_copy(src, dst, sem).start()

    def wait(ref, sem):
        pltpu.make_async_copy(ref, ref, sem).wait()

    barrier = pltpu.get_barrier_semaphore()

    def greet_px(t, _):
        pl.semaphore_signal(barrier, inc=1, device_id=at_px((a + t) % PX), device_id_type=MESH)
        return 0

    def greet_py(t, _):
        to = (b + t) % PY
        pl.semaphore_signal(barrier, inc=1, device_id=(a, to), device_id_type=MESH)
        return 0

    lax.fori_loop(1, PX, greet_px, 0)
    lax.fori_loop(1, PY, greet_py, 0)
    pl.semaphore_wait(barrier, PX - 1 + PY - 1)

    keep(stale, stale_all.at[a], r_stale.at[a])
    keep(send_idx.at[a], send_all.at[a], r_sidx.at[a])
    keep(recv_idx.at[:, b], recv_all.at[b], r_ridx.at[b])

    def start_stale(d, _):
        send(stale, stale_all.at[a], s_stale.at[d], r_stale.at[a], at_px((x + d) % SIDE * CORES + c))
        return 0

    def start_sidx(t, _):
        to = (a + t) % PX
        send(send_idx.at[to], send_all.at[a], s_sidx.at[t], r_sidx.at[a], at_px(to))
        return 0

    def start_ridx(t, _):
        to = (b + t) % PY
        send(recv_idx.at[:, to], recv_all.at[b], s_ridx.at[t], r_ridx.at[b], (a, to))
        return 0

    lax.fori_loop(1, PX, start_sidx, 0)
    lax.fori_loop(1, SIDE, start_stale, 0)
    lax.fori_loop(1, PY, start_ridx, 0)

    for k in GROUPS:
        def start_group(dy, _):
            dz = (dy + k) % SIDE
            to_y, to_z = (y + dy) % SIDE, (z + dz) % SIDE
            from_y, from_z = (y + SIDE - dy) % SIDE, (z + SIDE - dz) % SIDE

            @pl.when(dy + dz > 0)
            def _():
                send(adj_in.at[:, to_y, to_z], a_in.at[y, z], s_in.at[dy, dz], r_in.at[y, z], at_py(to_y, to_z))

            def start_out(t, _):
                to = (a + t) % PX
                send(
                    adj_out.at[to, from_y, from_z], a_out.at[a, from_y, from_z],
                    s_out.at[t, k], r_out.at[a, k], at_px(to),
                )
                return 0

            lax.fori_loop(1, PX, start_out, 0)
            keep(adj_out.at[a, from_y, from_z], a_out.at[a, from_y, from_z], r_out.at[a, k])
            return 0

        lax.fori_loop(0, SIDE, start_group, 0)
    keep(adj_in.at[:, y, z], a_in.at[y, z], r_in.at[y, z])

    def wait_sidx(i, _):
        wait(send_all.at[i], r_sidx.at[i])
        return 0

    def wait_ridx(j, _):
        wait(recv_all.at[j], r_ridx.at[j])
        return 0

    lax.fori_loop(0, PX, wait_sidx, 0)
    lax.fori_loop(0, PY, wait_ridx, 0)

    def gather(i):
        def body(py, _):
            index = send_all[i, py]
            hot = jnp.concatenate([hot_rows(index[k : k + 1]) for k in range(SIDE)], axis=0)
            rows = dot(hot, stale_all[i]).astype(BF16)
            for k in range(SIDE):
                rows_buf[py, k, i] = rows[k * SLOT : (k + 1) * SLOT]
            return 0

        lax.fori_loop(0, SIDE, body, 0)

    def near(d, _):
        i = (x + d) % SIDE * CORES + c
        wait(stale_all.at[i], r_stale.at[i])
        send(stale_all.at[i], stale_all.at[i], s_fwd.at[d], r_stale.at[i], at_px(x * CORES + other))
        gather(i)
        return 0

    def far(d, _):
        i = (x + d) % SIDE * CORES + other
        wait(stale_all.at[i], r_stale.at[i])
        gather(i)
        return 0

    lax.fori_loop(0, SIDE, near, 0)
    lax.fori_loop(0, SIDE, far, 0)

    total[...] = dot(local_adj[...], feats[...])

    def forward(py, pz):
        wait(a_in.at[py, pz], r_in.at[py, pz])
        p_b = py * SIDE + pz
        p = a * PY + p_b
        index = recv_all[p_b]
        same = p_b == b
        for i in range(PX):
            mine = jnp.full((SLOT, SLOT), owner[p, i * PY + b], jnp.int32) == 1
            block = jnp.where(mine, a_in[py, pz, i].astype(F32), a_out[i, py, pz].astype(F32))
            drop = jnp.full((SLOT, SLOT), jnp.where(same & (a == i), 1, 0), jnp.int32) == 1
            block = jnp.where(drop, 0.0, block).astype(BF16)
            a_in[py, pz, i] = block
            sums_buf[pl.ds(i * SLOT, SLOT)] = dot(block, rows_buf[py, pz, i]).astype(BF16)
        for r in range(2):
            hot = jnp.concatenate(
                [hot_columns(index[i : i + 1], r * FEAT, FEAT) for i in range(PX)], axis=1
            )
            part = dot(hot, sums_buf[...]).astype(BF16)
            part_z[py, pz, pl.ds(r * FEAT, FEAT)] = part[:, :HALF]
            part_y[py, pz, pl.ds(r * FEAT, FEAT)] = part[:, HALF:]

    def second_z(py):
        def arrive(d, _):
            f = (z + d) % SIDE
            wait(recv_z.at[py, f], r_z.at[py, f])
            return 0

        lax.fori_loop(1, SIDE, arrive, 0)
        acc = part_z[py, z].astype(F32)
        for d in range(1, SIDE):
            acc = acc + recv_z[py, (z + d) % SIDE].astype(F32)
        return acc

    def second_y(pz):
        def arrive(d, _):
            f = (y + d) % SIDE
            wait(recv_y.at[f, pz], r_y.at[f, pz])
            return 0

        lax.fori_loop(1, SIDE, arrive, 0)
        acc = part_y[y, pz].astype(F32)
        for d in range(1, SIDE):
            acc = acc + recv_y[(y + d) % SIDE, pz].astype(F32)
        return acc

    for k in GROUPS:

        def wait_out(i, _):
            wait(a_out.at[i, 0], r_out.at[i, k])
            return 0

        lax.fori_loop(0, PX, wait_out, 0)

        def step(dy, _):
            dz = (dy + k) % SIDE
            py, pz = (y + SIDE - dy) % SIDE, (z + SIDE - dz) % SIDE
            forward(py, pz)

            @pl.when(dz > 0)
            def _():
                send(part_z.at[py, pz], recv_z.at[py, z], s_z.at[dy, dz], r_z.at[py, z], at_py(y, pz))

            @pl.when(dy > 0)
            def _():
                send(part_y.at[py, pz], recv_y.at[y, pz], s_y.at[dy, dz], r_y.at[y, pz], at_py(py, z))

            return 0

        lax.fori_loop(0, SIDE, step, 0)

    def start_second(d, _):
        to_y, to_z = (y + d) % SIDE, (z + d) % SIDE
        send_z2[to_y] = second_z(to_y).astype(BF16)
        send(send_z2.at[to_y], recv_z2.at[y], s_z2.at[d], r_z2.at[y], at_py(to_y, z))
        send_y2[to_z] = second_y(to_z).astype(BF16)
        send(send_y2.at[to_z], recv_y2.at[z], s_y2.at[d], r_y2.at[z], at_py(y, to_z))
        return 0

    lax.fori_loop(1, SIDE, start_second, 0)
    total_y = second_y(z)
    total_z = second_z(y)
    for d in range(1, SIDE):
        f = (y + d) % SIDE
        wait(recv_z2.at[f], r_z2.at[f])
        total_z = total_z + recv_z2[f].astype(F32)
    total[:, :HALF] = total[:, :HALF] + total_z
    for d in range(1, SIDE):
        f = (z + d) % SIDE
        wait(recv_y2.at[f], r_y2.at[f])
        total_y = total_y + recv_y2[f].astype(F32)
    total[:, HALF:] = total[:, HALF:] + total_y

    summed = total[...].astype(BF16)
    pre = dot(summed, weight[...])
    pre_grad = gelu_grad(pre, cotangent[...].astype(F32)).astype(BF16)
    grad = dot(pre_grad, weight[...], 1, 1).astype(BF16)
    g_z[y, z] = grad[:, :HALF]
    g_y[y, z] = grad[:, HALF:]

    def on_ring(along_z, d):
        return at_py(y, (z + d) % SIDE) if along_z else at_py((y + d) % SIDE, z)

    def push(half, along_z, py, pz, slot):
        g, s_sem, r_sem = (g_z, s_gz, r_gz) if half == 0 else (g_y, s_gy, r_gy)
        for n in range(2):
            send(g.at[py, pz], g.at[py, pz], s_sem.at[slot, n], r_sem.at[py, pz, 0], on_ring(along_z, 1 + 2 * n))

    def pass_on(half, along_z, py, pz, slot, n):
        g, s_sem, r_sem = (g_z, s_hz, r_gz) if half == 0 else (g_y, s_hy, r_gy)
        part = g.at[py, pz, pl.ds(n * FEAT, FEAT)]
        send(part, part, s_sem.at[slot, n], r_sem.at[py, pz, n], on_ring(along_z, 1 + 2 * n))

    def got(half, py, pz):
        g, r_sem = (g_z, r_gz) if half == 0 else (g_y, r_gy)
        wait(g.at[py, pz], r_sem.at[py, pz, 0])

    def got_parts(half, py, pz):
        g, r_sem = (g_z, r_gz) if half == 0 else (g_y, r_gy)
        for n in range(2):
            wait(g.at[py, pz, pl.ds(n * FEAT, FEAT)], r_sem.at[py, pz, n])

    push(0, True, y, z, 0)
    push(1, False, y, z, 0)
    push(0, False, y, z, 1)
    push(1, True, y, z, 1)

    w_term[...] = dot(summed, pre_grad, 0, 0).reshape(PY, PART, FEAT)

    out_feats[...] = jax.nn.gelu(pre).astype(BF16)
    feat_grad[...] = dot(local_adj[...], grad, 0, 0).astype(BF16)

    def backward(py, pz):
        index = recv_all[py * SIDE + pz]
        grad_p = jnp.concatenate([g_z[py, pz], g_y[py, pz]], axis=1)
        for h in range(2):
            hot = jnp.concatenate([hot_rows(index[i : i + 1]) for i in range(h * 4, h * 4 + 4)], axis=0)
            rows = dot(hot, grad_p).astype(BF16)
            for k in range(4):
                i = h * 4 + k
                rows_buf[py, pz, i] = dot(
                    a_in[py, pz, i], rows[k * SLOT : (k + 1) * SLOT], 0, 0
                ).astype(BF16)

    backward(y, z)

    def near_first(n, _):
        f_z, f_y = (z + 3 - 2 * n) % SIDE, (y + 3 - 2 * n) % SIDE
        got(0, y, f_z)
        pass_on(0, True, y, f_z, 0, n)
        push(0, False, y, f_z, 2 + n)
        got(1, f_y, z)
        pass_on(1, False, f_y, z, 0, n)
        push(1, True, f_y, z, 2 + n)
        return 0

    def near_second(n, _):
        f_z, f_y = (z + 3 - 2 * n) % SIDE, (y + 3 - 2 * n) % SIDE
        got(1, y, f_z)
        pass_on(1, True, y, f_z, 1, n)
        got(0, f_y, z)
        pass_on(0, False, f_y, z, 1, n)
        return 0

    def near_z(n, _):
        backward(y, (z + 3 - 2 * n) % SIDE)
        return 0

    def near_y(n, _):
        backward((y + 3 - 2 * n) % SIDE, z)
        return 0

    far_y, far_z = (y + 2) % SIDE, (z + 2) % SIDE
    lax.fori_loop(0, 2, near_first, 0)
    lax.fori_loop(0, 2, near_second, 0)
    lax.fori_loop(0, 1, near_z, 0)
    got_parts(0, y, far_z)
    push(0, False, y, far_z, 4)
    got_parts(1, far_y, z)
    push(1, True, far_y, z, 4)

    def start_w(t, _):
        to = (b + t) % PY
        send(w_term.at[to], w_parts.at[b], s_w.at[t], r_w.at[b], (a, to))
        return 0

    lax.fori_loop(1, PY, start_w, 0)
    lax.fori_loop(1, 2, near_z, 0)

    def corners(t, _):
        n, m = t // 2, t % 2
        near, e = 3 - 2 * n, 3 - 2 * m
        got(0, (y + near) % SIDE, (z + e) % SIDE)
        pass_on(0, False, (y + near) % SIDE, (z + e) % SIDE, 2 + m, n)
        got(1, (y + e) % SIDE, (z + near) % SIDE)
        pass_on(1, True, (y + e) % SIDE, (z + near) % SIDE, 2 + m, n)
        return 0

    def edges(n, _):
        near = 3 - 2 * n
        got(0, (y + near) % SIDE, far_z)
        pass_on(0, False, (y + near) % SIDE, far_z, 4, n)
        got(1, far_y, (z + near) % SIDE)
        pass_on(1, True, far_y, (z + near) % SIDE, 4, n)
        return 0

    lax.fori_loop(0, 4, corners, 0)
    lax.fori_loop(0, 2, near_y, 0)
    lax.fori_loop(0, 2, edges, 0)

    def corner(t, _):
        backward((y + 3 - 2 * (t // 2)) % SIDE, (z + 3 - 2 * (t % 2)) % SIDE)
        return 0

    lax.fori_loop(0, 4, corner, 0)

    w_sum[a] = w_term[b]

    def add_w(t, _):
        f = (b + t) % PY
        wait(w_parts.at[f], r_w.at[f])
        w_sum[a] = w_sum[a] + w_parts[f]
        return 0

    lax.fori_loop(1, PY, add_w, 0)

    def start_w2(t, _):
        send(w_sum.at[a], w_parts2.at[a], s_w2.at[t], r_w2.at[a], at_px((a + t) % PX))
        return 0

    lax.fori_loop(1, PX, start_w2, 0)

    def edge_z(n, _):
        f_y = (y + 3 - 2 * n) % SIDE
        got_parts(1, f_y, far_z)
        backward(f_y, far_z)
        return 0

    def edge_y(n, _):
        f_z = (z + 3 - 2 * n) % SIDE
        got_parts(0, far_y, f_z)
        backward(far_y, f_z)
        return 0

    got_parts(1, y, far_z)
    backward(y, far_z)
    got_parts(0, far_y, z)
    backward(far_y, z)
    lax.fori_loop(0, 2, edge_z, 0)

    w_parts2[a] = w_sum[a]

    def wait_w2(t, _):
        f = (a + t) % PX
        wait(w_parts2.at[f], r_w2.at[f])
        return 0

    lax.fori_loop(1, PX, wait_w2, 0)
    acc = w_parts2[0]
    for i in range(1, PX):
        acc = acc + w_parts2[i]
    w_all[b] = acc * F32(1.0 / (PX * PY * ROWS) ** 0.5)

    def start_w3(t, _):
        to = (b + t) % PY
        send(w_all.at[b], w_all.at[b], s_w3.at[t], r_w3.at[b], (a, to))
        return 0

    lax.fori_loop(1, PY, start_w3, 0)
    lax.fori_loop(0, 2, edge_y, 0)
    got_parts(0, far_y, far_z)
    got_parts(1, far_y, far_z)
    backward(far_y, far_z)

    def scatter(i):
        acc = jnp.zeros((ROWS, FEAT), F32)
        for py in range(SIDE):
            index = send_all[i, py]
            hot = jnp.concatenate([hot_columns(index[k : k + 1], 0, ROWS) for k in range(SIDE)], axis=1)
            rows = jnp.concatenate([rows_buf[py, k, i] for k in range(SIDE)], axis=0)
            acc = acc + dot(hot, rows)
        return acc

    def start_core(d, _):
        to_x = (x + d) % SIDE
        bound_core[to_x] = scatter(to_x * CORES + other).astype(BF16)
        send(bound_core.at[to_x], recv_core.at[to_x], s_core.at[d], r_core.at[to_x], at_px(x * CORES + other))
        return 0

    lax.fori_loop(0, SIDE, start_core, 0)

    def start_x(d, _):
        to_x = (x + d) % SIDE
        acc = scatter(to_x * CORES + c)
        wait(recv_core.at[to_x], r_core.at[to_x])
        bound_x[to_x] = (acc + recv_core[to_x].astype(F32)).astype(BF16)
        send(bound_x.at[to_x], recv_x.at[x], s_x.at[d], r_x.at[x], at_px(to_x * CORES + c))
        return 0

    lax.fori_loop(1, SIDE, start_x, 0)
    acc = scatter(a)
    wait(recv_core.at[x], r_core.at[x])
    acc = acc + recv_core[x].astype(F32)

    def wait_w3(t, _):
        f = (b + t) % PY
        wait(w_all.at[f], r_w3.at[f])
        return 0

    lax.fori_loop(1, PY, wait_w3, 0)
    weight_grad[...] = w_all[...].reshape(FEAT, FEAT)

    for d in range(1, SIDE):
        f = (x + d) % SIDE
        wait(recv_x.at[f], r_x.at[f])
        acc = acc + recv_x[f].astype(F32)
    bound_grad[...] = acc.astype(BF16)

    def done_px(t, _):
        wait(send_all.at[0], s_sidx.at[t])
        for k in range(SIDE):
            wait(a_out.at[0, 0], s_out.at[t, k])
        wait(w_sum.at[0], s_w2.at[t])
        return 0

    def done_py(t, _):
        wait(recv_all.at[0], s_ridx.at[t])
        wait(w_term.at[0], s_w.at[t])
        wait(w_all.at[0], s_w3.at[t])
        return 0

    def done_in(t, _):
        wait(a_in.at[0, 0], s_in.at[t // SIDE, t % SIDE])
        return 0

    def done_side(d, _):
        wait(stale_all.at[0], s_stale.at[d])
        for k in range(SIDE):
            wait(part_z.at[0, 0], s_z.at[k, d])
            wait(part_y.at[0, 0], s_y.at[d, k])
        wait(send_z2.at[0], s_z2.at[d])
        wait(send_y2.at[0], s_y2.at[d])
        wait(bound_x.at[0], s_x.at[d])
        return 0

    def done_core(d, _):
        wait(stale_all.at[0], s_fwd.at[d])
        wait(bound_core.at[0], s_core.at[d])
        return 0

    def done_g(t, _):
        k, n = t // 2, t % 2
        wait(g_z.at[0, 0], s_gz.at[k, n])
        wait(g_y.at[0, 0], s_gy.at[k, n])
        wait(g_z.at[0, 0, pl.ds(0, FEAT)], s_hz.at[k, n])
        wait(g_y.at[0, 0, pl.ds(0, FEAT)], s_hy.at[k, n])
        return 0

    lax.fori_loop(0, 10, done_g, 0)
    lax.fori_loop(1, PX, done_px, 0)
    lax.fori_loop(1, PY, done_py, 0)
    lax.fori_loop(1, PY, done_in, 0)
    lax.fori_loop(1, SIDE, done_side, 0)
    lax.fori_loop(0, SIDE, done_core, 0)


def hand_over(*refs):
    count = len(refs) // 2
    for source, result in zip(refs[:count], refs[count:]):
        result[...] = source[...]


def on_device(
    feats, stale_feats, local_adj, adj_in, adj_out, owner, send_idx, recv_idx, weight, cotangent
):
    hbm = pl.BlockSpec(memory_space=pl.ANY)
    vmem = pl.BlockSpec(memory_space=pltpu.VMEM)
    dma = lambda *shape: pltpu.SemaphoreType.DMA(shape)
    node = lambda *shape: pltpu.VMEM((*shape, ROWS, HALF), BF16)
    shapes = (
        jax.ShapeDtypeStruct((ROWS, FEAT), BF16),
        jax.ShapeDtypeStruct((ROWS, FEAT), BF16),
        jax.ShapeDtypeStruct((ROWS, FEAT), BF16),
        jax.ShapeDtypeStruct((FEAT, FEAT), F32),
    )
    results = pl.pallas_call(
        kernel,
        out_shape=shapes,
        in_specs=[hbm] * 5 + [pl.BlockSpec(memory_space=pltpu.SMEM)] + [vmem] * 4,
        out_specs=(vmem,) * 4,
        scratch_shapes=[
            pltpu.VMEM((SIDE, SIDE, PX, SLOT, SLOT), BF16),
            pltpu.VMEM((PX, SIDE, SIDE, SLOT, SLOT), BF16),
            pltpu.VMEM((PX, ROWS, FEAT), BF16),
            pltpu.VMEM((PX, SIDE, SIDE, SLOT), jnp.int32),
            pltpu.VMEM((PY, PX, SLOT), jnp.int32),
            pltpu.VMEM((SIDE, SIDE, PX, SLOT, FEAT), BF16),
            pltpu.VMEM((PX * SLOT, FEAT), BF16),
            node(SIDE, SIDE),
            node(SIDE, SIDE),
            node(SIDE, SIDE),
            node(SIDE, SIDE),
            node(SIDE),
            node(SIDE),
            node(SIDE),
            node(SIDE),
            pltpu.VMEM((ROWS, FEAT), F32),
            node(SIDE, SIDE),
            node(SIDE, SIDE),
            pltpu.VMEM((SIDE, ROWS, FEAT), BF16),
            pltpu.VMEM((SIDE, ROWS, FEAT), BF16),
            pltpu.VMEM((SIDE, ROWS, FEAT), BF16),
            pltpu.VMEM((SIDE, ROWS, FEAT), BF16),
            pltpu.VMEM((PY, PART, FEAT), F32),
            pltpu.VMEM((PY, PART, FEAT), F32),
            pltpu.VMEM((PX, PART, FEAT), F32),
            pltpu.VMEM((PX, PART, FEAT), F32),
            pltpu.VMEM((PY, PART, FEAT), F32),
            dma(PY), dma(PY), dma(PX), dma(PX),
            dma(SIDE), dma(PX), dma(SIDE),
            dma(PX, SIDE), dma(PX, SIDE), dma(SIDE, SIDE), dma(SIDE, SIDE),
            dma(SIDE, SIDE), dma(SIDE, SIDE), dma(SIDE, SIDE), dma(SIDE, SIDE),
            dma(SIDE), dma(SIDE), dma(SIDE), dma(SIDE),
            dma(SIDE + 1, 2), dma(SIDE, SIDE, 2), dma(SIDE + 1, 2), dma(SIDE, SIDE, 2),
            dma(SIDE + 1, 2), dma(SIDE + 1, 2),
            dma(SIDE), dma(SIDE), dma(SIDE), dma(SIDE),
            dma(PY), dma(PY), dma(PX), dma(PX), dma(PY), dma(PY),
        ],
        compiler_params=pltpu.CompilerParams(
            collective_id=0, has_side_effects=True, vmem_limit_bytes=60 * 2**20
        ),
    )(
        adj_in.reshape(PX, SIDE, SIDE, SLOT, SLOT),
        adj_out.reshape(PX, SIDE, SIDE, SLOT, SLOT),
        stale_feats,
        send_idx.reshape(PX, SIDE, SIDE, SLOT),
        recv_idx.reshape(PX, PY, SLOT),
        owner,
        feats,
        local_adj,
        weight,
        cotangent,
    )
    return pl.pallas_call(
        hand_over, out_shape=shapes, in_specs=[vmem] * 4, out_specs=(vmem,) * 4
    )(*results)


def solution(mesh):
    both = ("px", "py")
    in_specs = (
        P(both, None),
        P(both, None),
        P(both, None),
        P(both, None, None),
        P(both, None, None),
        P(),
        P(both, None),
        P(both, None),
        P(),
        P(both, None),
    )
    out_specs = (P(both, None), P(both, None), P(both, None), P())
    return jax.shard_map(
        on_device, mesh=mesh, in_specs=in_specs, out_specs=out_specs, check_vma=False
    )
```

```python
import functools

import jax
import jax.numpy as jnp
from jax import lax
from jax.experimental import pallas as pl
from jax.experimental.pallas import tpu as pltpu
from jax.sharding import PartitionSpec as P

F32 = jnp.float32
BF16 = jnp.bfloat16
MESH = pl.DeviceIdType.MESH
PX, PY, CORES, SIDE = 8, 16, 2, 4
SLOT, ROWS, FEAT = 128, 512, 256
HALF = FEAT // 2
PART = FEAT // PY
GROUPS = (2, 1, 3, 0)


def gelu_grad(pre, grad):
    return jax.vjp(jax.nn.gelu, pre)[1](grad)[0]


def dot(left, right, left_dim=1, right_dim=0):
    return lax.dot_general(
        left, right, (((left_dim,), (right_dim,)), ((), ())), preferred_element_type=F32
    )


def hot_rows(index):
    column = jnp.broadcast_to(index.astype(F32), (SLOT, SLOT)).T
    lane = lax.broadcasted_iota(jnp.int32, (SLOT, SLOT), 1).astype(F32)
    return jnp.concatenate(
        [jnp.where(column == lane + F32(t * SLOT), 1.0, 0.0).astype(BF16) for t in range(ROWS // SLOT)],
        axis=1,
    )


def hot_columns(index, first, count):
    row = lax.broadcasted_iota(jnp.int32, (count, SLOT), 0) + first
    return jnp.where(row == index, 1.0, 0.0).astype(BF16)


def kernel(
    adj_in, adj_out, stale, send_idx, recv_idx, owner, feats, local_adj, weight, cotangent,
    out_feats, feat_grad, bound_grad, weight_grad,
    a_in, a_out, stale_all, send_all, recv_all, rows_buf, sums_buf, part_z, part_y, recv_z, recv_y, half_z, half_y,
    send_z2, send_y2, recv_z2, recv_y2, total, g_z, g_y, bound_core, bound_x, recv_core, recv_x,
    w_term, w_parts, w_sum, w_parts2, w_all,
    s_ridx, r_ridx, s_sidx, r_sidx, s_stale, r_stale, s_fwd, s_out, r_out, s_in, r_in,
    s_z, r_z, s_y, r_y, s_hz1, r_hz1, s_hy1, r_hy1, s_z2, r_z2, s_y2, r_y2,
    s_gz, r_gz, s_gy, r_gy, s_hz, s_hy, s_core, r_core, s_x, r_x, s_w, r_w, s_w2, r_w2, s_w3, r_w3,
):
    a, b = lax.axis_index("px"), lax.axis_index("py")
    x, c = a // CORES, a % CORES
    y, z = b // SIDE, b % SIDE
    other = 1 - c

    def at_px(to):
        return (to, b)

    def at_py(to_y, to_z):
        return (a, to_y * SIDE + to_z)

    def send(src, dst, s_sem, r_sem, to):
        pltpu.make_async_remote_copy(
            src_ref=src, dst_ref=dst, send_sem=s_sem, recv_sem=r_sem, device_id=to, device_id_type=MESH
        ).start()

    def keep(src, dst, sem):
        pltpu.make_async_copy(src, dst, sem).start()

    def wait(ref, sem):
        pltpu.make_async_copy(ref, ref, sem).wait()

    def on_ring(along_z, d):
        return at_py(y, (z + d) % SIDE) if along_z else at_py((y + d) % SIDE, z)

    barrier = pltpu.get_barrier_semaphore()

    def greet_px(t, _):
        pl.semaphore_signal(barrier, inc=1, device_id=at_px((a + t) % PX), device_id_type=MESH)
        return 0

    def greet_py(t, _):
        to = (b + t) % PY
        pl.semaphore_signal(barrier, inc=1, device_id=(a, to), device_id_type=MESH)
        return 0

    lax.fori_loop(1, PX, greet_px, 0)
    lax.fori_loop(1, PY, greet_py, 0)
    keep(stale, stale_all.at[a], r_stale.at[a])
    keep(send_idx.at[a], send_all.at[a], r_sidx.at[a])
    keep(recv_idx.at[:, b], recv_all.at[b], r_ridx.at[b])
    pl.semaphore_wait(barrier, PX - 1 + PY - 1)

    def start_stale(d, _):
        to = (x + d) % SIDE * CORES + c
        send(stale, stale_all.at[a], s_stale.at[d], r_stale.at[a], at_px(to))
        return 0

    def start_sidx(t, _):
        to = (a + t) % PX
        send(send_idx.at[to], send_all.at[a], s_sidx.at[t], r_sidx.at[a], at_px(to))
        return 0

    def start_ridx(t, _):
        to = (b + t) % PY
        send(recv_idx.at[:, to], recv_all.at[b], s_ridx.at[t], r_ridx.at[b], (a, to))
        return 0

    lax.fori_loop(1, PX, start_sidx, 0)
    lax.fori_loop(1, SIDE, start_stale, 0)
    lax.fori_loop(1, PY, start_ridx, 0)

    def start_blocks(k, ins=True, outs=True):
        def start_group(dy, _):
            dz = (dy + k) % SIDE
            to_y, to_z = (y + dy) % SIDE, (z + dz) % SIDE
            from_y, from_z = (y + SIDE - dy) % SIDE, (z + SIDE - dz) % SIDE

            @pl.when((dy + dz > 0) & ins)
            def _():
                send(adj_in.at[:, to_y, to_z], a_in.at[y, z], s_in.at[dy, dz], r_in.at[y, z], at_py(to_y, to_z))

            if not outs:
                return 0

            def start_out(t, _):
                to = (a + t) % PX
                send(
                    adj_out.at[to, from_y, from_z], a_out.at[a, from_y, from_z],
                    s_out.at[t, k], r_out.at[a, k], at_px(to),
                )
                return 0

            lax.fori_loop(1, PX, start_out, 0)
            keep(adj_out.at[a, from_y, from_z], a_out.at[a, from_y, from_z], r_out.at[a, k])
            return 0

        lax.fori_loop(0, SIDE, start_group, 0)

    start_blocks(GROUPS[0], True, False)
    keep(adj_in.at[:, y, z], a_in.at[y, z], r_in.at[y, z])

    def to_partner(i, d):
        send(stale_all.at[i], stale_all.at[i], s_fwd.at[d], r_stale.at[i], at_px(x * CORES + other))

    def near(d, _):
        i = (x + d) % SIDE * CORES + c
        wait(stale_all.at[i], r_stale.at[i])
        to_partner(i, d)
        return 0

    wait(stale_all.at[a], r_stale.at[a])
    to_partner(a, 0)
    lax.fori_loop(1, SIDE, near, 0)
    start_blocks(GROUPS[0], False, True)
    for k in GROUPS[1:]:
        start_blocks(k)

    def wait_sidx(i, _):
        wait(send_all.at[i], r_sidx.at[i])
        return 0

    def wait_ridx(j, _):
        wait(recv_all.at[j], r_ridx.at[j])
        return 0

    lax.fori_loop(0, PX, wait_sidx, 0)
    lax.fori_loop(0, PY, wait_ridx, 0)

    def gather(i):
        def body(py, _):
            index = send_all[i, py]
            hot = jnp.concatenate([hot_rows(index[k : k + 1]) for k in range(SIDE)], axis=0)
            rows = dot(hot, stale_all[i]).astype(BF16)
            for k in range(SIDE):
                rows_buf[py, k, i] = rows[k * SLOT : (k + 1) * SLOT]
            return 0

        lax.fori_loop(0, SIDE, body, 0)

    def own_rows(d, _):
        gather((x + d) % SIDE * CORES + c)
        return 0

    def partner_rows(d, _):
        i = (x + d) % SIDE * CORES + other
        wait(stale_all.at[i], r_stale.at[i])
        gather(i)
        return 0

    lax.fori_loop(0, SIDE, own_rows, 0)
    lax.fori_loop(0, SIDE, partner_rows, 0)

    total[...] = dot(local_adj[...], feats[...])

    def forward(py, pz):
        wait(a_in.at[py, pz], r_in.at[py, pz])
        p_b = py * SIDE + pz
        p = a * PY + p_b
        index = recv_all[p_b]
        same = p_b == b
        for i in range(PX):
            mine = jnp.full((SLOT, SLOT), owner[p, i * PY + b], jnp.int32) == 1
            block = jnp.where(mine, a_in[py, pz, i].astype(F32), a_out[i, py, pz].astype(F32))
            drop = jnp.full((SLOT, SLOT), jnp.where(same & (a == i), 1, 0), jnp.int32) == 1
            block = jnp.where(drop, 0.0, block).astype(BF16)
            a_in[py, pz, i] = block
            sums_buf[pl.ds(i * SLOT, SLOT)] = dot(block, rows_buf[py, pz, i]).astype(BF16)
        for r in range(2):
            hot = jnp.concatenate(
                [hot_columns(index[i : i + 1], r * FEAT, FEAT) for i in range(PX)], axis=1
            )
            part = dot(hot, sums_buf[...]).astype(BF16)
            part_z[py, pz, pl.ds(r * FEAT, FEAT)] = part[:, :HALF]
            part_y[py, pz, pl.ds(r * FEAT, FEAT)] = part[:, HALF:]

    def to_opposite(along_z, py, pz, slot):
        part, got, s_sem, r_sem = (part_z, half_z, s_hz1, r_hz1) if along_z else (part_y, half_y, s_hy1, r_hy1)
        row = py if along_z else pz
        for n in range(2):
            send(
                part.at[py, pz, pl.ds(n * FEAT, FEAT)], got.at[row, n],
                s_sem.at[slot, n], r_sem.at[row, n], on_ring(along_z, 1 + 2 * n),
            )

    def to_neighbour(along_z, n, py, pz, slot):
        part, got, r_got = (part_z, half_z, r_hz1) if along_z else (part_y, half_y, r_hy1)
        end, s_sem, r_sem = (recv_z, s_z, r_z) if along_z else (recv_y, s_y, r_y)
        row = py if along_z else pz
        wait(got.at[row, n], r_got.at[row, n])
        rows = pl.ds(n * FEAT, FEAT)
        part[py, pz, rows] = (part[py, pz, rows].astype(F32) + got[row, n].astype(F32)).astype(BF16)
        send(part.at[py, pz], end.at[row, n], s_sem.at[slot, n], r_sem.at[row, n], on_ring(along_z, 1 + 2 * n))

    def neighbours(items):
        for d, e in items:
            n = 0 if e == 3 else 1
            to_neighbour(True, n, (y + SIDE - d) % SIDE, (z + SIDE - e) % SIDE, d)
            to_neighbour(False, n, (y + SIDE - e) % SIDE, (z + SIDE - d) % SIDE, d)

    def second_z(py):
        acc = part_z[py, z].astype(F32)
        for n in range(2):
            wait(recv_z.at[py, n], r_z.at[py, n])
            acc = acc + recv_z[py, n].astype(F32)
        return acc

    def second_y(pz):
        acc = part_y[y, pz].astype(F32)
        for n in range(2):
            wait(recv_y.at[pz, n], r_y.at[pz, n])
            acc = acc + recv_y[pz, n].astype(F32)
        return acc

    for k in GROUPS:

        def wait_out(i, _):
            wait(a_out.at[i, 0], r_out.at[i, k])
            return 0

        lax.fori_loop(0, PX, wait_out, 0)

        def step(dy, _):
            dz = (dy + k) % SIDE
            py, pz = (y + SIDE - dy) % SIDE, (z + SIDE - dz) % SIDE
            forward(py, pz)

            @pl.when(dz == 2)
            def _():
                to_opposite(True, py, pz, dy)

            @pl.when(dy == 2)
            def _():
                to_opposite(False, py, pz, dz)

            return 0

        lax.fori_loop(0, SIDE, step, 0)
        if k == GROUPS[2]:
            neighbours(((1, 3), (0, 3), (3, 1), (0, 1)))

    neighbours(((2, 3), (2, 1), (3, 3), (1, 1)))

    def start_second(d, _):
        to_y, to_z = (y + d) % SIDE, (z + d) % SIDE
        send_z2[to_y] = second_z(to_y).astype(BF16)
        send(send_z2.at[to_y], recv_z2.at[y], s_z2.at[d], r_z2.at[y], at_py(to_y, z))
        send_y2[to_z] = second_y(to_z).astype(BF16)
        send(send_y2.at[to_z], recv_y2.at[z], s_y2.at[d], r_y2.at[z], at_py(y, to_z))
        return 0

    lax.fori_loop(1, SIDE, start_second, 0)
    total_y = second_y(z)
    total_z = second_z(y)
    for d in range(1, SIDE):
        f = (y + d) % SIDE
        wait(recv_z2.at[f], r_z2.at[f])
        total_z = total_z + recv_z2[f].astype(F32)
    total[:, :HALF] = total[:, :HALF] + total_z
    for d in range(1, SIDE):
        f = (z + d) % SIDE
        wait(recv_y2.at[f], r_y2.at[f])
        total_y = total_y + recv_y2[f].astype(F32)
    total[:, HALF:] = total[:, HALF:] + total_y

    summed = total[...].astype(BF16)
    pre = dot(summed, weight[...])
    pre_grad = gelu_grad(pre, cotangent[...].astype(F32)).astype(BF16)
    grad = dot(pre_grad, weight[...], 1, 1).astype(BF16)
    g_z[y, z] = grad[:, :HALF]
    g_y[y, z] = grad[:, HALF:]

    def push(half, along_z, py, pz, slot):
        g, s_sem, r_sem = (g_z, s_gz, r_gz) if half == 0 else (g_y, s_gy, r_gy)
        for n in range(2):
            send(g.at[py, pz], g.at[py, pz], s_sem.at[slot, n], r_sem.at[py, pz, 0], on_ring(along_z, 1 + 2 * n))

    def pass_on(half, along_z, py, pz, slot, n):
        g, s_sem, r_sem = (g_z, s_hz, r_gz) if half == 0 else (g_y, s_hy, r_gy)
        part = g.at[py, pz, pl.ds(n * FEAT, FEAT)]
        send(part, part, s_sem.at[slot, n], r_sem.at[py, pz, n], on_ring(along_z, 1 + 2 * n))

    def got(half, py, pz):
        g, r_sem = (g_z, r_gz) if half == 0 else (g_y, r_gy)
        wait(g.at[py, pz], r_sem.at[py, pz, 0])

    def got_parts(half, py, pz):
        g, r_sem = (g_z, r_gz) if half == 0 else (g_y, r_gy)
        for n in range(2):
            wait(g.at[py, pz, pl.ds(n * FEAT, FEAT)], r_sem.at[py, pz, n])

    push(0, True, y, z, 0)
    push(1, False, y, z, 0)
    push(0, False, y, z, 1)
    push(1, True, y, z, 1)

    w_term[...] = dot(summed, pre_grad, 0, 0).reshape(PY, PART, FEAT)

    out_feats[...] = jax.nn.gelu(pre).astype(BF16)
    feat_grad[...] = dot(local_adj[...], grad, 0, 0).astype(BF16)

    def backward(py, pz):
        index = recv_all[py * SIDE + pz]
        grad_p = jnp.concatenate([g_z[py, pz], g_y[py, pz]], axis=1)
        for h in range(2):
            hot = jnp.concatenate([hot_rows(index[i : i + 1]) for i in range(h * 4, h * 4 + 4)], axis=0)
            rows = dot(hot, grad_p).astype(BF16)
            for k in range(4):
                i = h * 4 + k
                rows_buf[py, pz, i] = dot(
                    a_in[py, pz, i], rows[k * SLOT : (k + 1) * SLOT], 0, 0
                ).astype(BF16)

    backward(y, z)

    def near_first(n, _):
        f_z, f_y = (z + 3 - 2 * n) % SIDE, (y + 3 - 2 * n) % SIDE
        got(0, y, f_z)
        pass_on(0, True, y, f_z, 0, n)
        push(0, False, y, f_z, 2 + n)
        got(1, f_y, z)
        pass_on(1, False, f_y, z, 0, n)
        push(1, True, f_y, z, 2 + n)
        return 0

    def near_second(n, _):
        f_z, f_y = (z + 3 - 2 * n) % SIDE, (y + 3 - 2 * n) % SIDE
        got(1, y, f_z)
        pass_on(1, True, y, f_z, 1, n)
        got(0, f_y, z)
        pass_on(0, False, f_y, z, 1, n)
        return 0

    def near_z(n, _):
        backward(y, (z + 3 - 2 * n) % SIDE)
        return 0

    def near_y(n, _):
        backward((y + 3 - 2 * n) % SIDE, z)
        return 0

    far_y, far_z = (y + 2) % SIDE, (z + 2) % SIDE
    lax.fori_loop(0, 2, near_first, 0)
    lax.fori_loop(0, 2, near_second, 0)
    lax.fori_loop(0, 1, near_z, 0)
    got_parts(0, y, far_z)
    push(0, False, y, far_z, 4)
    got_parts(1, far_y, z)
    push(1, True, far_y, z, 4)

    def start_w(t, _):
        to = (b + t) % PY
        send(w_term.at[to], w_parts.at[b], s_w.at[t], r_w.at[b], (a, to))
        return 0

    lax.fori_loop(1, PY, start_w, 0)
    lax.fori_loop(1, 2, near_z, 0)

    def corners(t, _):
        n, m = t // 2, t % 2
        near, e = 3 - 2 * n, 3 - 2 * m
        got(0, (y + near) % SIDE, (z + e) % SIDE)
        pass_on(0, False, (y + near) % SIDE, (z + e) % SIDE, 2 + m, n)
        got(1, (y + e) % SIDE, (z + near) % SIDE)
        pass_on(1, True, (y + e) % SIDE, (z + near) % SIDE, 2 + m, n)
        return 0

    def edges(n, _):
        near = 3 - 2 * n
        got(0, (y + near) % SIDE, far_z)
        pass_on(0, False, (y + near) % SIDE, far_z, 4, n)
        got(1, far_y, (z + near) % SIDE)
        pass_on(1, True, far_y, (z + near) % SIDE, 4, n)
        return 0

    lax.fori_loop(0, 4, corners, 0)
    lax.fori_loop(0, 2, near_y, 0)
    lax.fori_loop(0, 2, edges, 0)

    def corner(t, _):
        backward((y + 3 - 2 * (t // 2)) % SIDE, (z + 3 - 2 * (t % 2)) % SIDE)
        return 0

    lax.fori_loop(0, 4, corner, 0)

    w_sum[a] = w_term[b]

    def add_w(t, _):
        f = (b + t) % PY
        wait(w_parts.at[f], r_w.at[f])
        w_sum[a] = w_sum[a] + w_parts[f]
        return 0

    lax.fori_loop(1, PY, add_w, 0)

    def start_w2(t, _):
        send(w_sum.at[a], w_parts2.at[a], s_w2.at[t], r_w2.at[a], at_px((a + t) % PX))
        return 0

    lax.fori_loop(1, PX, start_w2, 0)

    def edge_z(n, _):
        f_y = (y + 3 - 2 * n) % SIDE
        got_parts(1, f_y, far_z)
        backward(f_y, far_z)
        return 0

    def edge_y(n, _):
        f_z = (z + 3 - 2 * n) % SIDE
        got_parts(0, far_y, f_z)
        backward(far_y, f_z)
        return 0

    got_parts(1, y, far_z)
    backward(y, far_z)
    got_parts(0, far_y, z)
    backward(far_y, z)
    lax.fori_loop(0, 2, edge_z, 0)

    w_parts2[a] = w_sum[a]

    def wait_w2(t, _):
        f = (a + t) % PX
        wait(w_parts2.at[f], r_w2.at[f])
        return 0

    lax.fori_loop(1, PX, wait_w2, 0)
    acc = w_parts2[0]
    for i in range(1, PX):
        acc = acc + w_parts2[i]
    w_all[b] = acc * F32(1.0 / (PX * PY * ROWS) ** 0.5)

    def start_w3(t, _):
        to = (b + t) % PY
        send(w_all.at[b], w_all.at[b], s_w3.at[t], r_w3.at[b], (a, to))
        return 0

    lax.fori_loop(1, PY, start_w3, 0)
    lax.fori_loop(0, 2, edge_y, 0)
    got_parts(0, far_y, far_z)
    got_parts(1, far_y, far_z)
    backward(far_y, far_z)

    def scatter(i):
        acc = jnp.zeros((ROWS, FEAT), F32)
        for py in range(SIDE):
            index = send_all[i, py]
            hot = jnp.concatenate([hot_columns(index[k : k + 1], 0, ROWS) for k in range(SIDE)], axis=1)
            rows = jnp.concatenate([rows_buf[py, k, i] for k in range(SIDE)], axis=0)
            acc = acc + dot(hot, rows)
        return acc

    def start_core(d, _):
        to_x = (x + d) % SIDE
        bound_core[to_x] = scatter(to_x * CORES + other).astype(BF16)
        send(bound_core.at[to_x], recv_core.at[to_x], s_core.at[d], r_core.at[to_x], at_px(x * CORES + other))
        return 0

    lax.fori_loop(0, SIDE, start_core, 0)

    def start_x(d, _):
        to_x = (x + d) % SIDE
        acc = scatter(to_x * CORES + c)
        wait(recv_core.at[to_x], r_core.at[to_x])
        bound_x[to_x] = (acc + recv_core[to_x].astype(F32)).astype(BF16)
        send(bound_x.at[to_x], recv_x.at[x], s_x.at[d], r_x.at[x], at_px(to_x * CORES + c))
        return 0

    lax.fori_loop(1, SIDE, start_x, 0)
    acc = scatter(a)
    wait(recv_core.at[x], r_core.at[x])
    acc = acc + recv_core[x].astype(F32)

    def wait_w3(t, _):
        f = (b + t) % PY
        wait(w_all.at[f], r_w3.at[f])
        return 0

    lax.fori_loop(1, PY, wait_w3, 0)
    weight_grad[...] = w_all[...].reshape(FEAT, FEAT)

    for d in range(1, SIDE):
        f = (x + d) % SIDE
        wait(recv_x.at[f], r_x.at[f])
        acc = acc + recv_x[f].astype(F32)
    bound_grad[...] = acc.astype(BF16)

    def done_px(t, _):
        wait(send_all.at[0], s_sidx.at[t])
        for k in range(SIDE):
            wait(a_out.at[0, 0], s_out.at[t, k])
        wait(w_sum.at[0], s_w2.at[t])
        return 0

    def done_py(t, _):
        wait(recv_all.at[0], s_ridx.at[t])
        wait(w_term.at[0], s_w.at[t])
        wait(w_all.at[0], s_w3.at[t])
        return 0

    def done_in(t, _):
        wait(a_in.at[0, 0], s_in.at[t // SIDE, t % SIDE])
        return 0

    def done_side(d, _):
        wait(stale_all.at[0], s_stale.at[d])
        wait(send_z2.at[0], s_z2.at[d])
        wait(send_y2.at[0], s_y2.at[d])
        wait(bound_x.at[0], s_x.at[d])
        return 0

    def done_core(d, _):
        wait(stale_all.at[0], s_fwd.at[d])
        wait(bound_core.at[0], s_core.at[d])
        return 0

    def done_g(t, _):
        k, n = t // 2, t % 2
        wait(g_z.at[0, 0], s_gz.at[k, n])
        wait(g_y.at[0, 0], s_gy.at[k, n])
        wait(g_z.at[0, 0, pl.ds(0, FEAT)], s_hz.at[k, n])
        wait(g_y.at[0, 0, pl.ds(0, FEAT)], s_hy.at[k, n])
        return 0

    def done_sums(t, _):
        k, n = t // 2, t % 2
        wait(part_z.at[0, 0], s_z.at[k, n])
        wait(part_y.at[0, 0], s_y.at[k, n])
        wait(part_z.at[0, 0, pl.ds(0, FEAT)], s_hz1.at[k, n])
        wait(part_y.at[0, 0, pl.ds(0, FEAT)], s_hy1.at[k, n])
        return 0

    lax.fori_loop(0, 8, done_sums, 0)
    lax.fori_loop(0, 10, done_g, 0)
    lax.fori_loop(1, PX, done_px, 0)
    lax.fori_loop(1, PY, done_py, 0)
    lax.fori_loop(1, PY, done_in, 0)
    lax.fori_loop(1, SIDE, done_side, 0)
    lax.fori_loop(0, SIDE, done_core, 0)


def hand_over(*refs):
    count = len(refs) // 2
    for source, result in zip(refs[:count], refs[count:]):
        result[...] = source[...]


def on_device(
    feats, stale_feats, local_adj, adj_in, adj_out, owner, send_idx, recv_idx, weight, cotangent
):
    hbm = pl.BlockSpec(memory_space=pl.ANY)
    vmem = pl.BlockSpec(memory_space=pltpu.VMEM)
    dma = lambda *shape: pltpu.SemaphoreType.DMA(shape)
    node = lambda *shape: pltpu.VMEM((*shape, ROWS, HALF), BF16)
    shapes = (
        jax.ShapeDtypeStruct((ROWS, FEAT), BF16),
        jax.ShapeDtypeStruct((ROWS, FEAT), BF16),
        jax.ShapeDtypeStruct((ROWS, FEAT), BF16),
        jax.ShapeDtypeStruct((FEAT, FEAT), F32),
    )
    results = pl.pallas_call(
        kernel,
        out_shape=shapes,
        in_specs=[hbm] * 5 + [pl.BlockSpec(memory_space=pltpu.SMEM)] + [vmem] * 4,
        out_specs=(vmem,) * 4,
        scratch_shapes=[
            pltpu.VMEM((SIDE, SIDE, PX, SLOT, SLOT), BF16),
            pltpu.VMEM((PX, SIDE, SIDE, SLOT, SLOT), BF16),
            pltpu.VMEM((PX, ROWS, FEAT), BF16),
            pltpu.VMEM((PX, SIDE, SIDE, SLOT), jnp.int32),
            pltpu.VMEM((PY, PX, SLOT), jnp.int32),
            pltpu.VMEM((SIDE, SIDE, PX, SLOT, FEAT), BF16),
            pltpu.VMEM((PX * SLOT, FEAT), BF16),
            node(SIDE, SIDE),
            node(SIDE, SIDE),
            node(SIDE, 2),
            node(SIDE, 2),
            pltpu.VMEM((SIDE, 2, FEAT, HALF), BF16),
            pltpu.VMEM((SIDE, 2, FEAT, HALF), BF16),
            node(SIDE),
            node(SIDE),
            node(SIDE),
            node(SIDE),
            pltpu.VMEM((ROWS, FEAT), F32),
            node(SIDE, SIDE),
            node(SIDE, SIDE),
            pltpu.VMEM((SIDE, ROWS, FEAT), BF16),
            pltpu.VMEM((SIDE, ROWS, FEAT), BF16),
            pltpu.VMEM((SIDE, ROWS, FEAT), BF16),
            pltpu.VMEM((SIDE, ROWS, FEAT), BF16),
            pltpu.VMEM((PY, PART, FEAT), F32),
            pltpu.VMEM((PY, PART, FEAT), F32),
            pltpu.VMEM((PX, PART, FEAT), F32),
            pltpu.VMEM((PX, PART, FEAT), F32),
            pltpu.VMEM((PY, PART, FEAT), F32),
            dma(PY), dma(PY), dma(PX), dma(PX),
            dma(SIDE), dma(PX), dma(SIDE),
            dma(PX, SIDE), dma(PX, SIDE), dma(SIDE, SIDE), dma(SIDE, SIDE),
            dma(SIDE, 2), dma(SIDE, 2), dma(SIDE, 2), dma(SIDE, 2),
            dma(SIDE, 2), dma(SIDE, 2), dma(SIDE, 2), dma(SIDE, 2),
            dma(SIDE), dma(SIDE), dma(SIDE), dma(SIDE),
            dma(SIDE + 1, 2), dma(SIDE, SIDE, 2), dma(SIDE + 1, 2), dma(SIDE, SIDE, 2),
            dma(SIDE + 1, 2), dma(SIDE + 1, 2),
            dma(SIDE), dma(SIDE), dma(SIDE), dma(SIDE),
            dma(PY), dma(PY), dma(PX), dma(PX), dma(PY), dma(PY),
        ],
        compiler_params=pltpu.CompilerParams(
            collective_id=0, has_side_effects=True, vmem_limit_bytes=60 * 2**20
        ),
    )(
        adj_in.reshape(PX, SIDE, SIDE, SLOT, SLOT),
        adj_out.reshape(PX, SIDE, SIDE, SLOT, SLOT),
        stale_feats,
        send_idx.reshape(PX, SIDE, SIDE, SLOT),
        recv_idx.reshape(PX, PY, SLOT),
        owner,
        feats,
        local_adj,
        weight,
        cotangent,
    )
    return pl.pallas_call(
        hand_over, out_shape=shapes, in_specs=[vmem] * 4, out_specs=(vmem,) * 4
    )(*results)


def solution(mesh):
    both = ("px", "py")
    in_specs = (
        P(both, None),
        P(both, None),
        P(both, None),
        P(both, None, None),
        P(both, None, None),
        P(),
        P(both, None),
        P(both, None),
        P(),
        P(both, None),
    )
    out_specs = (P(both, None), P(both, None), P(both, None), P())
    return jax.shard_map(
        on_device, mesh=mesh, in_specs=in_specs, out_specs=out_specs, check_vma=False
    )
```

```python
import functools

import jax
import jax.numpy as jnp
from jax import lax
from jax.experimental import pallas as pl
from jax.experimental.pallas import tpu as pltpu
from jax.sharding import PartitionSpec as P

F32 = jnp.float32
BF16 = jnp.bfloat16
MESH = pl.DeviceIdType.MESH
PX, PY, CORES, SIDE = 8, 16, 2, 4
SLOT, ROWS, FEAT = 128, 512, 256
HALF = FEAT // 2
PART = FEAT // PY
GROUPS = (2, 1, 3, 0)


def gelu_grad(pre, grad):
    return jax.vjp(jax.nn.gelu, pre)[1](grad)[0]


def dot(left, right, left_dim=1, right_dim=0):
    return lax.dot_general(
        left, right, (((left_dim,), (right_dim,)), ((), ())), preferred_element_type=F32
    )


def hot_rows(index):
    column = jnp.broadcast_to(index.astype(F32), (SLOT, SLOT)).T
    lane = lax.broadcasted_iota(jnp.int32, (SLOT, SLOT), 1).astype(F32)
    return jnp.concatenate(
        [jnp.where(column == lane + F32(t * SLOT), 1.0, 0.0).astype(BF16) for t in range(ROWS // SLOT)],
        axis=1,
    )


def hot_columns(index, first, count):
    row = lax.broadcasted_iota(jnp.int32, (count, SLOT), 0) + first
    return jnp.where(row == index, 1.0, 0.0).astype(BF16)


def kernel(
    adj_in, adj_out, stale, send_idx, recv_idx, owner, feats, local_adj, weight, cotangent,
    out_feats, feat_grad, bound_grad, weight_grad,
    a_in, a_out, stale_all, send_all, recv_all, rows_buf, sums_buf, part_z, part_y, recv_z, recv_y, half_z, half_y,
    send_z2, send_y2, recv_z2, recv_y2, total, g_z, g_y, bound_core, bound_x, recv_core, recv_x,
    w_term, w_parts, w_sum, w_parts2, w_all, hot_recv,
    s_ridx, r_ridx, s_sidx, r_sidx, s_stale, r_stale, s_fwd, s_out, r_out, s_in, r_in,
    s_z, r_z, s_y, r_y, s_hz1, r_hz1, s_hy1, r_hy1, s_z2, r_z2, s_y2, r_y2,
    s_gz, r_gz, s_gy, r_gy, s_hz, s_hy, s_core, r_core, s_x, r_x, s_w, r_w, s_w2, r_w2, s_w3, r_w3,
):
    a, b = lax.axis_index("px"), lax.axis_index("py")
    x, c = a // CORES, a % CORES
    y, z = b // SIDE, b % SIDE
    other = 1 - c

    def at_px(to):
        return (to, b)

    def at_py(to_y, to_z):
        return (a, to_y * SIDE + to_z)

    def send(src, dst, s_sem, r_sem, to):
        pltpu.make_async_remote_copy(
            src_ref=src, dst_ref=dst, send_sem=s_sem, recv_sem=r_sem, device_id=to, device_id_type=MESH
        ).start()

    def keep(src, dst, sem):
        pltpu.make_async_copy(src, dst, sem).start()

    def wait(ref, sem):
        pltpu.make_async_copy(ref, ref, sem).wait()

    def on_ring(along_z, d):
        return at_py(y, (z + d) % SIDE) if along_z else at_py((y + d) % SIDE, z)

    barrier = pltpu.get_barrier_semaphore()

    def greet_px(t, _):
        pl.semaphore_signal(barrier, inc=1, device_id=at_px((a + t) % PX), device_id_type=MESH)
        return 0

    def greet_py(t, _):
        to = (b + t) % PY
        pl.semaphore_signal(barrier, inc=1, device_id=(a, to), device_id_type=MESH)
        return 0

    lax.fori_loop(1, PX, greet_px, 0)
    lax.fori_loop(1, PY, greet_py, 0)
    keep(stale, stale_all.at[a], r_stale.at[a])
    keep(send_idx.at[a], send_all.at[a], r_sidx.at[a])
    keep(recv_idx.at[:, b], recv_all.at[b], r_ridx.at[b])
    pl.semaphore_wait(barrier, PX - 1 + PY - 1)

    def start_stale(d, _):
        to = (x + d) % SIDE * CORES + c
        send(stale, stale_all.at[a], s_stale.at[d], r_stale.at[a], at_px(to))
        return 0

    def start_sidx(t, _):
        to = (a + t) % PX
        send(send_idx.at[to], send_all.at[a], s_sidx.at[t], r_sidx.at[a], at_px(to))
        return 0

    def start_ridx(t, _):
        to = (b + t) % PY
        send(recv_idx.at[:, to], recv_all.at[b], s_ridx.at[t], r_ridx.at[b], (a, to))
        return 0

    lax.fori_loop(1, PX, start_sidx, 0)
    lax.fori_loop(1, SIDE, start_stale, 0)
    lax.fori_loop(1, PY, start_ridx, 0)

    def start_blocks(k, ins=True, outs=True):
        def start_group(dy, _):
            dz = (dy + k) % SIDE
            to_y, to_z = (y + dy) % SIDE, (z + dz) % SIDE
            from_y, from_z = (y + SIDE - dy) % SIDE, (z + SIDE - dz) % SIDE

            @pl.when((dy + dz > 0) & ins)
            def _():
                send(adj_in.at[:, to_y, to_z], a_in.at[y, z], s_in.at[dy, dz], r_in.at[y, z], at_py(to_y, to_z))

            if not outs:
                return 0

            def start_out(t, _):
                to = (a + t) % PX
                send(
                    adj_out.at[to, from_y, from_z], a_out.at[a, from_y, from_z],
                    s_out.at[t, k], r_out.at[a, k], at_px(to),
                )
                return 0

            lax.fori_loop(1, PX, start_out, 0)
            keep(adj_out.at[a, from_y, from_z], a_out.at[a, from_y, from_z], r_out.at[a, k])
            return 0

        lax.fori_loop(0, SIDE, start_group, 0)

    start_blocks(GROUPS[0], True, False)
    start_blocks(GROUPS[1], True, False)
    keep(adj_in.at[:, y, z], a_in.at[y, z], r_in.at[y, z])

    def to_partner(i, d):
        send(stale_all.at[i], stale_all.at[i], s_fwd.at[d], r_stale.at[i], at_px(x * CORES + other))

    def near(d, _):
        i = (x + d) % SIDE * CORES + c
        wait(stale_all.at[i], r_stale.at[i])
        to_partner(i, d)
        return 0

    wait(stale_all.at[a], r_stale.at[a])
    to_partner(a, 0)
    lax.fori_loop(1, SIDE, near, 0)
    start_blocks(GROUPS[0], False, True)
    start_blocks(GROUPS[1], False, True)
    for k in GROUPS[2:]:
        start_blocks(k)

    def wait_sidx(i, _):
        wait(send_all.at[i], r_sidx.at[i])
        return 0

    def wait_ridx(j, _):
        wait(recv_all.at[j], r_ridx.at[j])
        return 0

    lax.fori_loop(0, PX, wait_sidx, 0)
    lax.fori_loop(0, PY, wait_ridx, 0)

    def gather(i):
        def body(py, _):
            index = send_all[i, py]
            hot = jnp.concatenate([hot_rows(index[k : k + 1]) for k in range(SIDE)], axis=0)
            rows = dot(hot, stale_all[i]).astype(BF16)
            for k in range(SIDE):
                rows_buf[py, k, i] = rows[k * SLOT : (k + 1) * SLOT]
            return 0

        lax.fori_loop(0, SIDE, body, 0)

    def own_rows(d, _):
        gather((x + d) % SIDE * CORES + c)
        return 0

    def partner_rows(d, _):
        i = (x + d) % SIDE * CORES + other
        wait(stale_all.at[i], r_stale.at[i])
        gather(i)
        return 0

    lax.fori_loop(0, SIDE, own_rows, 0)
    lax.fori_loop(0, SIDE, partner_rows, 0)

    def receivers(t, _):
        index = recv_all[t]
        for i in range(PX):
            hot_recv[t, pl.ds(i * SLOT, SLOT)] = hot_rows(index[i : i + 1])
        return 0

    lax.fori_loop(0, PY, receivers, 0)
    total[...] = dot(local_adj[...], feats[...])

    def forward(py, pz):
        wait(a_in.at[py, pz], r_in.at[py, pz])
        p_b = py * SIDE + pz
        p = a * PY + p_b
        index = recv_all[p_b]
        same = p_b == b
        for i in range(PX):
            mine = jnp.full((SLOT, SLOT), owner[p, i * PY + b], jnp.int32) == 1
            block = jnp.where(mine, a_in[py, pz, i].astype(F32), a_out[i, py, pz].astype(F32))
            drop = jnp.full((SLOT, SLOT), jnp.where(same & (a == i), 1, 0), jnp.int32) == 1
            block = jnp.where(drop, 0.0, block).astype(BF16)
            a_in[py, pz, i] = block
            sums_buf[pl.ds(i * SLOT, SLOT)] = dot(block, rows_buf[py, pz, i]).astype(BF16)
        for r in range(2):
            hot = jnp.concatenate(
                [hot_columns(index[i : i + 1], r * FEAT, FEAT) for i in range(PX)], axis=1
            )
            part = dot(hot, sums_buf[...]).astype(BF16)
            part_z[py, pz, pl.ds(r * FEAT, FEAT)] = part[:, :HALF]
            part_y[py, pz, pl.ds(r * FEAT, FEAT)] = part[:, HALF:]

    def to_opposite(along_z, py, pz, slot):
        part, got, s_sem, r_sem = (part_z, half_z, s_hz1, r_hz1) if along_z else (part_y, half_y, s_hy1, r_hy1)
        row = py if along_z else pz
        for n in range(2):
            send(
                part.at[py, pz, pl.ds(n * FEAT, FEAT)], got.at[row, n],
                s_sem.at[slot, n], r_sem.at[row, n], on_ring(along_z, 1 + 2 * n),
            )

    def to_neighbour(along_z, n, py, pz, slot):
        part, got, r_got = (part_z, half_z, r_hz1) if along_z else (part_y, half_y, r_hy1)
        end, s_sem, r_sem = (recv_z, s_z, r_z) if along_z else (recv_y, s_y, r_y)
        row = py if along_z else pz
        wait(got.at[row, n], r_got.at[row, n])
        rows = pl.ds(n * FEAT, FEAT)
        part[py, pz, rows] = (part[py, pz, rows].astype(F32) + got[row, n].astype(F32)).astype(BF16)
        send(part.at[py, pz], end.at[row, n], s_sem.at[slot, n], r_sem.at[row, n], on_ring(along_z, 1 + 2 * n))

    def neighbours(items):
        for d, e in items:
            n = 0 if e == 3 else 1
            to_neighbour(True, n, (y + SIDE - d) % SIDE, (z + SIDE - e) % SIDE, d)
            to_neighbour(False, n, (y + SIDE - e) % SIDE, (z + SIDE - d) % SIDE, d)

    def second_z(py):
        acc = part_z[py, z].astype(F32)
        for n in range(2):
            wait(recv_z.at[py, n], r_z.at[py, n])
            acc = acc + recv_z[py, n].astype(F32)
        return acc

    def second_y(pz):
        acc = part_y[y, pz].astype(F32)
        for n in range(2):
            wait(recv_y.at[pz, n], r_y.at[pz, n])
            acc = acc + recv_y[pz, n].astype(F32)
        return acc

    for k in GROUPS:

        def wait_out(i, _):
            wait(a_out.at[i, 0], r_out.at[i, k])
            return 0

        lax.fori_loop(0, PX, wait_out, 0)

        def step(t, _):
            dy = (t + 2) % SIDE
            dz = (dy + k) % SIDE
            py, pz = (y + SIDE - dy) % SIDE, (z + SIDE - dz) % SIDE
            forward(py, pz)

            @pl.when(dz == 2)
            def _():
                to_opposite(True, py, pz, dy)

            @pl.when(dy == 2)
            def _():
                to_opposite(False, py, pz, dz)

            return 0

        lax.fori_loop(0, SIDE, step, 0)
        if k == GROUPS[2]:
            neighbours(((1, 3), (0, 3), (3, 1), (0, 1)))

    neighbours(((2, 3), (2, 1), (3, 3), (1, 1)))

    def start_second(d, _):
        to_y, to_z = (y + d) % SIDE, (z + d) % SIDE
        send_z2[to_y] = second_z(to_y).astype(BF16)
        send(send_z2.at[to_y], recv_z2.at[y], s_z2.at[d], r_z2.at[y], at_py(to_y, z))
        send_y2[to_z] = second_y(to_z).astype(BF16)
        send(send_y2.at[to_z], recv_y2.at[z], s_y2.at[d], r_y2.at[z], at_py(y, to_z))
        return 0

    lax.fori_loop(1, SIDE, start_second, 0)
    total_y = second_y(z)
    total_z = second_z(y)
    for d in range(1, SIDE):
        f = (y + d) % SIDE
        wait(recv_z2.at[f], r_z2.at[f])
        total_z = total_z + recv_z2[f].astype(F32)
    total[:, :HALF] = total[:, :HALF] + total_z
    for d in range(1, SIDE):
        f = (z + d) % SIDE
        wait(recv_y2.at[f], r_y2.at[f])
        total_y = total_y + recv_y2[f].astype(F32)
    total[:, HALF:] = total[:, HALF:] + total_y

    summed = total[...].astype(BF16)
    pre = dot(summed, weight[...])
    pre_grad = gelu_grad(pre, cotangent[...].astype(F32)).astype(BF16)
    grad = dot(pre_grad, weight[...], 1, 1).astype(BF16)
    g_z[y, z] = grad[:, :HALF]
    g_y[y, z] = grad[:, HALF:]

    def push(half, along_z, py, pz, slot):
        g, s_sem, r_sem = (g_z, s_gz, r_gz) if half == 0 else (g_y, s_gy, r_gy)
        for n in range(2):
            send(g.at[py, pz], g.at[py, pz], s_sem.at[slot, n], r_sem.at[py, pz, 0], on_ring(along_z, 1 + 2 * n))

    def pass_on(half, along_z, py, pz, slot, n):
        g, s_sem, r_sem = (g_z, s_hz, r_gz) if half == 0 else (g_y, s_hy, r_gy)
        part = g.at[py, pz, pl.ds(n * FEAT, FEAT)]
        send(part, part, s_sem.at[slot, n], r_sem.at[py, pz, n], on_ring(along_z, 1 + 2 * n))

    def got(half, py, pz):
        g, r_sem = (g_z, r_gz) if half == 0 else (g_y, r_gy)
        wait(g.at[py, pz], r_sem.at[py, pz, 0])

    def got_parts(half, py, pz):
        g, r_sem = (g_z, r_gz) if half == 0 else (g_y, r_gy)
        for n in range(2):
            wait(g.at[py, pz, pl.ds(n * FEAT, FEAT)], r_sem.at[py, pz, n])

    push(0, True, y, z, 0)
    push(1, False, y, z, 0)
    push(0, False, y, z, 1)
    push(1, True, y, z, 1)

    w_term[...] = dot(summed, pre_grad, 0, 0).reshape(PY, PART, FEAT)

    out_feats[...] = jax.nn.gelu(pre).astype(BF16)
    feat_grad[...] = dot(local_adj[...], grad, 0, 0).astype(BF16)

    def backward(py, pz):
        p_b = py * SIDE + pz
        grad_p = jnp.concatenate([g_z[py, pz], g_y[py, pz]], axis=1)
        for h in range(2):
            hot = hot_recv[p_b, pl.ds(h * 4 * SLOT, 4 * SLOT)]
            rows = dot(hot, grad_p).astype(BF16)
            for k in range(4):
                i = h * 4 + k
                rows_buf[py, pz, i] = dot(
                    a_in[py, pz, i], rows[k * SLOT : (k + 1) * SLOT], 0, 0
                ).astype(BF16)

    backward(y, z)

    def near_first(n, _):
        f_z, f_y = (z + 3 - 2 * n) % SIDE, (y + 3 - 2 * n) % SIDE
        got(0, y, f_z)
        pass_on(0, True, y, f_z, 0, n)
        push(0, False, y, f_z, 2 + n)
        got(1, f_y, z)
        pass_on(1, False, f_y, z, 0, n)
        push(1, True, f_y, z, 2 + n)
        return 0

    def near_second(n, _):
        f_z, f_y = (z + 3 - 2 * n) % SIDE, (y + 3 - 2 * n) % SIDE
        got(1, y, f_z)
        pass_on(1, True, y, f_z, 1, n)
        got(0, f_y, z)
        pass_on(0, False, f_y, z, 1, n)
        return 0

    def near_z(n, _):
        backward(y, (z + 3 - 2 * n) % SIDE)
        return 0

    def near_y(n, _):
        backward((y + 3 - 2 * n) % SIDE, z)
        return 0

    far_y, far_z = (y + 2) % SIDE, (z + 2) % SIDE
    lax.fori_loop(0, 2, near_first, 0)
    lax.fori_loop(0, 2, near_second, 0)
    lax.fori_loop(0, 1, near_z, 0)
    got_parts(0, y, far_z)
    push(0, False, y, far_z, 4)
    got_parts(1, far_y, z)
    push(1, True, far_y, z, 4)

    lax.fori_loop(1, 2, near_z, 0)

    def corners(t, _):
        n, m = t // 2, t % 2
        near, e = 3 - 2 * n, 3 - 2 * m
        got(0, (y + near) % SIDE, (z + e) % SIDE)
        pass_on(0, False, (y + near) % SIDE, (z + e) % SIDE, 2 + m, n)
        got(1, (y + e) % SIDE, (z + near) % SIDE)
        pass_on(1, True, (y + e) % SIDE, (z + near) % SIDE, 2 + m, n)
        return 0

    def edges(n, _):
        near = 3 - 2 * n
        got(0, (y + near) % SIDE, far_z)
        pass_on(0, False, (y + near) % SIDE, far_z, 4, n)
        got(1, far_y, (z + near) % SIDE)
        pass_on(1, True, far_y, (z + near) % SIDE, 4, n)
        return 0

    lax.fori_loop(0, 4, corners, 0)
    lax.fori_loop(0, 2, near_y, 0)
    lax.fori_loop(0, 2, edges, 0)

    def start_w(t, _):
        to = (b + t) % PY
        send(w_term.at[to], w_parts.at[b], s_w.at[t], r_w.at[b], (a, to))
        return 0

    lax.fori_loop(1, PY, start_w, 0)

    def corner(t, _):
        backward((y + 3 - 2 * (t // 2)) % SIDE, (z + 3 - 2 * (t % 2)) % SIDE)
        return 0

    lax.fori_loop(0, 4, corner, 0)

    def edge_z(n, _):
        f_y = (y + 3 - 2 * n) % SIDE
        got_parts(1, f_y, far_z)
        backward(f_y, far_z)
        return 0

    def edge_y(n, _):
        f_z = (z + 3 - 2 * n) % SIDE
        got_parts(0, far_y, f_z)
        backward(far_y, f_z)
        return 0

    got_parts(1, y, far_z)
    backward(y, far_z)
    got_parts(0, far_y, z)
    backward(far_y, z)
    lax.fori_loop(0, 2, edge_z, 0)

    lax.fori_loop(0, 2, edge_y, 0)
    got_parts(0, far_y, far_z)
    got_parts(1, far_y, far_z)
    backward(far_y, far_z)

    def scatter(i):
        acc = jnp.zeros((ROWS, FEAT), F32)
        for py in range(SIDE):
            index = send_all[i, py]
            hot = jnp.concatenate([hot_columns(index[k : k + 1], 0, ROWS) for k in range(SIDE)], axis=1)
            rows = jnp.concatenate([rows_buf[py, k, i] for k in range(SIDE)], axis=0)
            acc = acc + dot(hot, rows)
        return acc

    def start_core(d, _):
        to_x = (x + d) % SIDE
        bound_core[to_x] = scatter(to_x * CORES + other).astype(BF16)
        send(bound_core.at[to_x], recv_core.at[to_x], s_core.at[d], r_core.at[to_x], at_px(x * CORES + other))
        return 0

    lax.fori_loop(0, SIDE, start_core, 0)

    w_sum[a] = w_term[b]

    def add_w(t, _):
        f = (b + t) % PY
        wait(w_parts.at[f], r_w.at[f])
        w_sum[a] = w_sum[a] + w_parts[f]
        return 0

    lax.fori_loop(1, PY, add_w, 0)

    def start_w2(t, _):
        send(w_sum.at[a], w_parts2.at[a], s_w2.at[t], r_w2.at[a], at_px((a + t) % PX))
        return 0

    lax.fori_loop(1, PX, start_w2, 0)

    def start_x(t, _):
        d = (t + 1) % 3 + 1
        to_x = (x + d) % SIDE
        acc = scatter(to_x * CORES + c)
        wait(recv_core.at[to_x], r_core.at[to_x])
        bound_x[to_x] = (acc + recv_core[to_x].astype(F32)).astype(BF16)
        send(bound_x.at[to_x], recv_x.at[x], s_x.at[d], r_x.at[x], at_px(to_x * CORES + c))
        return 0

    lax.fori_loop(0, SIDE - 1, start_x, 0)

    w_parts2[a] = w_sum[a]

    def wait_w2(t, _):
        f = (a + t) % PX
        wait(w_parts2.at[f], r_w2.at[f])
        return 0

    lax.fori_loop(1, PX, wait_w2, 0)
    acc = w_parts2[0]
    for i in range(1, PX):
        acc = acc + w_parts2[i]
    w_all[b] = acc * F32(1.0 / (PX * PY * ROWS) ** 0.5)

    def start_w3(t, _):
        to = (b + t) % PY
        send(w_all.at[b], w_all.at[b], s_w3.at[t], r_w3.at[b], (a, to))
        return 0

    lax.fori_loop(1, PY, start_w3, 0)
    acc = scatter(a)
    wait(recv_core.at[x], r_core.at[x])
    acc = acc + recv_core[x].astype(F32)

    def wait_w3(t, _):
        f = (b + t) % PY
        wait(w_all.at[f], r_w3.at[f])
        return 0

    lax.fori_loop(1, PY, wait_w3, 0)
    weight_grad[...] = w_all[...].reshape(FEAT, FEAT)

    for d in range(1, SIDE):
        f = (x + d) % SIDE
        wait(recv_x.at[f], r_x.at[f])
        acc = acc + recv_x[f].astype(F32)
    bound_grad[...] = acc.astype(BF16)

    def done_px(t, _):
        wait(send_all.at[0], s_sidx.at[t])
        for k in range(SIDE):
            wait(a_out.at[0, 0], s_out.at[t, k])
        wait(w_sum.at[0], s_w2.at[t])
        return 0

    def done_py(t, _):
        wait(recv_all.at[0], s_ridx.at[t])
        wait(w_term.at[0], s_w.at[t])
        wait(w_all.at[0], s_w3.at[t])
        return 0

    def done_in(t, _):
        wait(a_in.at[0, 0], s_in.at[t // SIDE, t % SIDE])
        return 0

    def done_side(d, _):
        wait(stale_all.at[0], s_stale.at[d])
        wait(send_z2.at[0], s_z2.at[d])
        wait(send_y2.at[0], s_y2.at[d])
        wait(bound_x.at[0], s_x.at[d])
        return 0

    def done_core(d, _):
        wait(stale_all.at[0], s_fwd.at[d])
        wait(bound_core.at[0], s_core.at[d])
        return 0

    def done_g(t, _):
        k, n = t // 2, t % 2
        wait(g_z.at[0, 0], s_gz.at[k, n])
        wait(g_y.at[0, 0], s_gy.at[k, n])
        wait(g_z.at[0, 0, pl.ds(0, FEAT)], s_hz.at[k, n])
        wait(g_y.at[0, 0, pl.ds(0, FEAT)], s_hy.at[k, n])
        return 0

    def done_sums(t, _):
        k, n = t // 2, t % 2
        wait(part_z.at[0, 0], s_z.at[k, n])
        wait(part_y.at[0, 0], s_y.at[k, n])
        wait(part_z.at[0, 0, pl.ds(0, FEAT)], s_hz1.at[k, n])
        wait(part_y.at[0, 0, pl.ds(0, FEAT)], s_hy1.at[k, n])
        return 0

    lax.fori_loop(0, 8, done_sums, 0)
    lax.fori_loop(0, 10, done_g, 0)
    lax.fori_loop(1, PX, done_px, 0)
    lax.fori_loop(1, PY, done_py, 0)
    lax.fori_loop(1, PY, done_in, 0)
    lax.fori_loop(1, SIDE, done_side, 0)
    lax.fori_loop(0, SIDE, done_core, 0)


def hand_over(*refs):
    count = len(refs) // 2
    for source, result in zip(refs[:count], refs[count:]):
        result[...] = source[...]


def on_device(
    feats, stale_feats, local_adj, adj_in, adj_out, owner, send_idx, recv_idx, weight, cotangent
):
    hbm = pl.BlockSpec(memory_space=pl.ANY)
    vmem = pl.BlockSpec(memory_space=pltpu.VMEM)
    dma = lambda *shape: pltpu.SemaphoreType.DMA(shape)
    node = lambda *shape: pltpu.VMEM((*shape, ROWS, HALF), BF16)
    shapes = (
        jax.ShapeDtypeStruct((ROWS, FEAT), BF16),
        jax.ShapeDtypeStruct((ROWS, FEAT), BF16),
        jax.ShapeDtypeStruct((ROWS, FEAT), BF16),
        jax.ShapeDtypeStruct((FEAT, FEAT), F32),
    )
    results = pl.pallas_call(
        kernel,
        out_shape=shapes,
        in_specs=[hbm] * 5 + [pl.BlockSpec(memory_space=pltpu.SMEM)] + [vmem] * 4,
        out_specs=(vmem,) * 4,
        scratch_shapes=[
            pltpu.VMEM((SIDE, SIDE, PX, SLOT, SLOT), BF16),
            pltpu.VMEM((PX, SIDE, SIDE, SLOT, SLOT), BF16),
            pltpu.VMEM((PX, ROWS, FEAT), BF16),
            pltpu.VMEM((PX, SIDE, SIDE, SLOT), jnp.int32),
            pltpu.VMEM((PY, PX, SLOT), jnp.int32),
            pltpu.VMEM((SIDE, SIDE, PX, SLOT, FEAT), BF16),
            pltpu.VMEM((PX * SLOT, FEAT), BF16),
            node(SIDE, SIDE),
            node(SIDE, SIDE),
            node(SIDE, 2),
            node(SIDE, 2),
            pltpu.VMEM((SIDE, 2, FEAT, HALF), BF16),
            pltpu.VMEM((SIDE, 2, FEAT, HALF), BF16),
            node(SIDE),
            node(SIDE),
            node(SIDE),
            node(SIDE),
            pltpu.VMEM((ROWS, FEAT), F32),
            node(SIDE, SIDE),
            node(SIDE, SIDE),
            pltpu.VMEM((SIDE, ROWS, FEAT), BF16),
            pltpu.VMEM((SIDE, ROWS, FEAT), BF16),
            pltpu.VMEM((SIDE, ROWS, FEAT), BF16),
            pltpu.VMEM((SIDE, ROWS, FEAT), BF16),
            pltpu.VMEM((PY, PART, FEAT), F32),
            pltpu.VMEM((PY, PART, FEAT), F32),
            pltpu.VMEM((PX, PART, FEAT), F32),
            pltpu.VMEM((PX, PART, FEAT), F32),
            pltpu.VMEM((PY, PART, FEAT), F32),
            pltpu.VMEM((PY, PX * SLOT, ROWS), BF16),
            dma(PY), dma(PY), dma(PX), dma(PX),
            dma(SIDE), dma(PX), dma(SIDE),
            dma(PX, SIDE), dma(PX, SIDE), dma(SIDE, SIDE), dma(SIDE, SIDE),
            dma(SIDE, 2), dma(SIDE, 2), dma(SIDE, 2), dma(SIDE, 2),
            dma(SIDE, 2), dma(SIDE, 2), dma(SIDE, 2), dma(SIDE, 2),
            dma(SIDE), dma(SIDE), dma(SIDE), dma(SIDE),
            dma(SIDE + 1, 2), dma(SIDE, SIDE, 2), dma(SIDE + 1, 2), dma(SIDE, SIDE, 2),
            dma(SIDE + 1, 2), dma(SIDE + 1, 2),
            dma(SIDE), dma(SIDE), dma(SIDE), dma(SIDE),
            dma(PY), dma(PY), dma(PX), dma(PX), dma(PY), dma(PY),
        ],
        compiler_params=pltpu.CompilerParams(
            collective_id=0, has_side_effects=True, vmem_limit_bytes=60 * 2**20
        ),
    )(
        adj_in.reshape(PX, SIDE, SIDE, SLOT, SLOT),
        adj_out.reshape(PX, SIDE, SIDE, SLOT, SLOT),
        stale_feats,
        send_idx.reshape(PX, SIDE, SIDE, SLOT),
        recv_idx.reshape(PX, PY, SLOT),
        owner,
        feats,
        local_adj,
        weight,
        cotangent,
    )
    return pl.pallas_call(
        hand_over, out_shape=shapes, in_specs=[vmem] * 4, out_specs=(vmem,) * 4
    )(*results)


def solution(mesh):
    both = ("px", "py")
    in_specs = (
        P(both, None),
        P(both, None),
        P(both, None),
        P(both, None, None),
        P(both, None, None),
        P(),
        P(both, None),
        P(both, None),
        P(),
        P(both, None),
    )
    out_specs = (P(both, None), P(both, None), P(both, None), P())
    return jax.shard_map(
        on_device, mesh=mesh, in_specs=in_specs, out_specs=out_specs, check_vma=False
    )
```

```python
import functools

import jax
import jax.numpy as jnp
from jax import lax
from jax.experimental import pallas as pl
from jax.experimental.pallas import tpu as pltpu
from jax.sharding import PartitionSpec as P

F32 = jnp.float32
BF16 = jnp.bfloat16
MESH = pl.DeviceIdType.MESH
PX, PY, CORES, SIDE = 8, 16, 2, 4
SLOT, ROWS, FEAT = 128, 512, 256
HALF = FEAT // 2
PART = FEAT // PY
GROUPS = (2, 1, 3, 0)


def gelu_grad(pre, grad):
    return jax.vjp(jax.nn.gelu, pre)[1](grad)[0]


def dot(left, right, left_dim=1, right_dim=0):
    return lax.dot_general(
        left, right, (((left_dim,), (right_dim,)), ((), ())), preferred_element_type=F32
    )


def hot_rows(index):
    column = jnp.broadcast_to(index.astype(F32), (SLOT, SLOT)).T
    lane = lax.broadcasted_iota(jnp.int32, (SLOT, SLOT), 1).astype(F32)
    return jnp.concatenate(
        [jnp.where(column == lane + F32(t * SLOT), 1.0, 0.0).astype(BF16) for t in range(ROWS // SLOT)],
        axis=1,
    )


def hot_columns(index, first, count):
    row = lax.broadcasted_iota(jnp.int32, (count, SLOT), 0) + first
    return jnp.where(row == index, 1.0, 0.0).astype(BF16)


def kernel(
    adj_in, adj_out, stale, send_idx, recv_idx, owner, feats, local_adj, weight, cotangent,
    out_feats, feat_grad, bound_grad, weight_grad,
    a_in, a_out, stale_all, send_all, recv_all, rows_buf, sums_buf, part_z, part_y, recv_z, recv_y, half_z, half_y,
    send_z2, send_y2, recv_z2, recv_y2, total, g_z, g_y, bound_core, bound_x, recv_core, recv_x,
    w_term, w_parts, w_sum, w_parts2, w_all, hot_recv,
    s_ridx, r_ridx, s_sidx, r_sidx, s_stale, r_stale, s_fwd, s_out, r_out, s_in, r_in,
    s_z, r_z, s_y, r_y, s_hz1, r_hz1, s_hy1, r_hy1, s_z2, r_z2, s_y2, r_y2,
    s_gz, r_gz, s_gy, r_gy, s_hz, s_hy, s_core, r_core, s_x, r_x, s_w, r_w, s_w2, r_w2, s_w3, r_w3,
):
    a, b = lax.axis_index("px"), lax.axis_index("py")
    x, c = a // CORES, a % CORES
    y, z = b // SIDE, b % SIDE
    other = 1 - c

    def at_px(to):
        return (to, b)

    def at_py(to_y, to_z):
        return (a, to_y * SIDE + to_z)

    def send(src, dst, s_sem, r_sem, to):
        pltpu.make_async_remote_copy(
            src_ref=src, dst_ref=dst, send_sem=s_sem, recv_sem=r_sem, device_id=to, device_id_type=MESH
        ).start()

    def keep(src, dst, sem):
        pltpu.make_async_copy(src, dst, sem).start()

    def wait(ref, sem):
        pltpu.make_async_copy(ref, ref, sem).wait()

    def on_ring(along_z, d):
        return at_py(y, (z + d) % SIDE) if along_z else at_py((y + d) % SIDE, z)

    barrier = pltpu.get_barrier_semaphore()

    def greet_px(t, _):
        pl.semaphore_signal(barrier, inc=1, device_id=at_px((a + t) % PX), device_id_type=MESH)
        return 0

    def greet_py(t, _):
        to = (b + t) % PY
        pl.semaphore_signal(barrier, inc=1, device_id=(a, to), device_id_type=MESH)
        return 0

    lax.fori_loop(1, PX, greet_px, 0)
    lax.fori_loop(1, PY, greet_py, 0)
    keep(stale, stale_all.at[a], r_stale.at[a])
    keep(send_idx.at[a], send_all.at[a], r_sidx.at[a])
    keep(recv_idx.at[:, b], recv_all.at[b], r_ridx.at[b])
    pl.semaphore_wait(barrier, PX - 1 + PY - 1)

    def start_stale(d, _):
        to = (x + d) % SIDE * CORES + c
        send(stale, stale_all.at[a], s_stale.at[d], r_stale.at[a], at_px(to))
        return 0

    def start_sidx(t, _):
        to = (a + t) % PX
        send(send_idx.at[to], send_all.at[a], s_sidx.at[t], r_sidx.at[a], at_px(to))
        return 0

    def start_ridx(t, _):
        to = (b + t) % PY
        send(recv_idx.at[:, to], recv_all.at[b], s_ridx.at[t], r_ridx.at[b], (a, to))
        return 0

    lax.fori_loop(1, SIDE, start_stale, 0)
    lax.fori_loop(1, PX, start_sidx, 0)
    lax.fori_loop(1, PY, start_ridx, 0)

    def start_blocks(k, ins=True, outs=True):
        def start_group(dy, _):
            dz = (dy + k) % SIDE
            to_y, to_z = (y + dy) % SIDE, (z + dz) % SIDE
            from_y, from_z = (y + SIDE - dy) % SIDE, (z + SIDE - dz) % SIDE

            @pl.when((dy + dz > 0) & ins)
            def _():
                send(adj_in.at[:, to_y, to_z], a_in.at[y, z], s_in.at[dy, dz], r_in.at[y, z], at_py(to_y, to_z))

            if not outs:
                return 0

            def start_out(t, _):
                to = (a + t) % PX
                send(
                    adj_out.at[to, from_y, from_z], a_out.at[a, from_y, from_z],
                    s_out.at[t, k], r_out.at[a, k], at_px(to),
                )
                return 0

            lax.fori_loop(1, PX, start_out, 0)
            keep(adj_out.at[a, from_y, from_z], a_out.at[a, from_y, from_z], r_out.at[a, k])
            return 0

        lax.fori_loop(0, SIDE, start_group, 0)

    start_blocks(GROUPS[0], True, False)
    start_blocks(GROUPS[1], True, False)
    keep(adj_in.at[:, y, z], a_in.at[y, z], r_in.at[y, z])

    def to_partner(i, d):
        send(stale_all.at[i], stale_all.at[i], s_fwd.at[d], r_stale.at[i], at_px(x * CORES + other))

    def near(d, _):
        i = (x + d) % SIDE * CORES + c
        wait(stale_all.at[i], r_stale.at[i])
        to_partner(i, d)
        return 0

    wait(stale_all.at[a], r_stale.at[a])
    to_partner(a, 0)
    lax.fori_loop(1, SIDE, near, 0)
    start_blocks(GROUPS[0], False, True)
    start_blocks(GROUPS[1], False, True)
    for k in GROUPS[2:]:
        start_blocks(k)

    def wait_sidx(i, _):
        wait(send_all.at[i], r_sidx.at[i])
        return 0

    def wait_ridx(j, _):
        wait(recv_all.at[j], r_ridx.at[j])
        return 0

    lax.fori_loop(0, PX, wait_sidx, 0)
    lax.fori_loop(0, PY, wait_ridx, 0)

    def gather(i):
        def body(py, _):
            index = send_all[i, py]
            hot = jnp.concatenate([hot_rows(index[k : k + 1]) for k in range(SIDE)], axis=0)
            rows = dot(hot, stale_all[i]).astype(BF16)
            for k in range(SIDE):
                rows_buf[py, k, i] = rows[k * SLOT : (k + 1) * SLOT]
            return 0

        lax.fori_loop(0, SIDE, body, 0)

    def own_rows(d, _):
        gather((x + d) % SIDE * CORES + c)
        return 0

    def partner_rows(d, _):
        i = (x + d) % SIDE * CORES + other
        wait(stale_all.at[i], r_stale.at[i])
        gather(i)
        return 0

    lax.fori_loop(0, SIDE, own_rows, 0)
    lax.fori_loop(0, SIDE, partner_rows, 0)

    def receivers(t, _):
        index = recv_all[t]
        for i in range(PX):
            hot_recv[t, pl.ds(i * SLOT, SLOT)] = hot_rows(index[i : i + 1])
        return 0

    lax.fori_loop(0, PY, receivers, 0)
    total[...] = dot(local_adj[...], feats[...])

    def forward(py, pz):
        wait(a_in.at[py, pz], r_in.at[py, pz])
        p_b = py * SIDE + pz
        p = a * PY + p_b
        index = recv_all[p_b]
        same = p_b == b
        for i in range(PX):
            mine = jnp.full((SLOT, SLOT), owner[p, i * PY + b], jnp.int32) == 1
            block = jnp.where(mine, a_in[py, pz, i].astype(F32), a_out[i, py, pz].astype(F32))
            drop = jnp.full((SLOT, SLOT), jnp.where(same & (a == i), 1, 0), jnp.int32) == 1
            block = jnp.where(drop, 0.0, block).astype(BF16)
            a_in[py, pz, i] = block
            sums_buf[pl.ds(i * SLOT, SLOT)] = dot(block, rows_buf[py, pz, i]).astype(BF16)
        for r in range(2):
            hot = jnp.concatenate(
                [hot_columns(index[i : i + 1], r * FEAT, FEAT) for i in range(PX)], axis=1
            )
            part = dot(hot, sums_buf[...]).astype(BF16)
            part_z[py, pz, pl.ds(r * FEAT, FEAT)] = part[:, :HALF]
            part_y[py, pz, pl.ds(r * FEAT, FEAT)] = part[:, HALF:]

    def to_opposite(along_z, py, pz, slot):
        part, got, s_sem, r_sem = (part_z, half_z, s_hz1, r_hz1) if along_z else (part_y, half_y, s_hy1, r_hy1)
        row = py if along_z else pz
        for n in range(2):
            send(
                part.at[py, pz, pl.ds(n * FEAT, FEAT)], got.at[row, n],
                s_sem.at[slot, n], r_sem.at[row, n], on_ring(along_z, 1 + 2 * n),
            )

    def to_neighbour(along_z, n, py, pz, slot):
        part, got, r_got = (part_z, half_z, r_hz1) if along_z else (part_y, half_y, r_hy1)
        end, s_sem, r_sem = (recv_z, s_z, r_z) if along_z else (recv_y, s_y, r_y)
        row = py if along_z else pz
        wait(got.at[row, n], r_got.at[row, n])
        rows = pl.ds(n * FEAT, FEAT)
        part[py, pz, rows] = (part[py, pz, rows].astype(F32) + got[row, n].astype(F32)).astype(BF16)
        send(part.at[py, pz], end.at[row, n], s_sem.at[slot, n], r_sem.at[row, n], on_ring(along_z, 1 + 2 * n))

    def neighbours(items):
        for d, e in items:
            n = 0 if e == 3 else 1
            to_neighbour(True, n, (y + SIDE - d) % SIDE, (z + SIDE - e) % SIDE, d)
            to_neighbour(False, n, (y + SIDE - e) % SIDE, (z + SIDE - d) % SIDE, d)

    def second_z(py):
        acc = part_z[py, z].astype(F32)
        for n in range(2):
            wait(recv_z.at[py, n], r_z.at[py, n])
            acc = acc + recv_z[py, n].astype(F32)
        return acc

    def second_y(pz):
        acc = part_y[y, pz].astype(F32)
        for n in range(2):
            wait(recv_y.at[pz, n], r_y.at[pz, n])
            acc = acc + recv_y[pz, n].astype(F32)
        return acc

    for k in GROUPS:

        def wait_out(i, _):
            wait(a_out.at[i, 0], r_out.at[i, k])
            return 0

        lax.fori_loop(0, PX, wait_out, 0)

        def step(t, _):
            dy = (t + 2) % SIDE
            dz = (dy + k) % SIDE
            py, pz = (y + SIDE - dy) % SIDE, (z + SIDE - dz) % SIDE
            forward(py, pz)

            @pl.when(dz == 2)
            def _():
                to_opposite(True, py, pz, dy)

            @pl.when(dy == 2)
            def _():
                to_opposite(False, py, pz, dz)

            return 0

        lax.fori_loop(0, SIDE, step, 0)
        if k == GROUPS[2]:
            neighbours(((1, 3), (0, 3), (3, 1), (0, 1)))

    neighbours(((2, 3), (2, 1), (3, 3), (1, 1)))

    def start_second(d, _):
        to_y, to_z = (y + d) % SIDE, (z + d) % SIDE
        send_z2[to_y] = second_z(to_y).astype(BF16)
        send(send_z2.at[to_y], recv_z2.at[y], s_z2.at[d], r_z2.at[y], at_py(to_y, z))
        send_y2[to_z] = second_y(to_z).astype(BF16)
        send(send_y2.at[to_z], recv_y2.at[z], s_y2.at[d], r_y2.at[z], at_py(y, to_z))
        return 0

    lax.fori_loop(1, SIDE, start_second, 0)
    total_y = second_y(z)
    total_z = second_z(y)
    for d in range(1, SIDE):
        f = (y + d) % SIDE
        wait(recv_z2.at[f], r_z2.at[f])
        total_z = total_z + recv_z2[f].astype(F32)
    total[:, :HALF] = total[:, :HALF] + total_z
    for d in range(1, SIDE):
        f = (z + d) % SIDE
        wait(recv_y2.at[f], r_y2.at[f])
        total_y = total_y + recv_y2[f].astype(F32)
    total[:, HALF:] = total[:, HALF:] + total_y

    summed = total[...].astype(BF16)
    pre = dot(summed, weight[...])
    pre_grad = gelu_grad(pre, cotangent[...].astype(F32)).astype(BF16)
    grad = dot(pre_grad, weight[...], 1, 1).astype(BF16)
    g_z[y, z] = grad[:, :HALF]
    g_y[y, z] = grad[:, HALF:]

    def push(half, along_z, py, pz, slot):
        g, s_sem, r_sem = (g_z, s_gz, r_gz) if half == 0 else (g_y, s_gy, r_gy)
        for n in range(2):
            send(g.at[py, pz], g.at[py, pz], s_sem.at[slot, n], r_sem.at[py, pz, 0], on_ring(along_z, 1 + 2 * n))

    def pass_on(half, along_z, py, pz, slot, n):
        g, s_sem, r_sem = (g_z, s_hz, r_gz) if half == 0 else (g_y, s_hy, r_gy)
        part = g.at[py, pz, pl.ds(n * FEAT, FEAT)]
        send(part, part, s_sem.at[slot, n], r_sem.at[py, pz, n], on_ring(along_z, 1 + 2 * n))

    def got(half, py, pz):
        g, r_sem = (g_z, r_gz) if half == 0 else (g_y, r_gy)
        wait(g.at[py, pz], r_sem.at[py, pz, 0])

    def got_parts(half, py, pz):
        g, r_sem = (g_z, r_gz) if half == 0 else (g_y, r_gy)
        for n in range(2):
            wait(g.at[py, pz, pl.ds(n * FEAT, FEAT)], r_sem.at[py, pz, n])

    push(0, True, y, z, 0)
    push(1, False, y, z, 0)
    push(0, False, y, z, 1)
    push(1, True, y, z, 1)

    w_term[...] = dot(summed, pre_grad, 0, 0).reshape(PY, PART, FEAT)

    out_feats[...] = jax.nn.gelu(pre).astype(BF16)
    feat_grad[...] = dot(local_adj[...], grad, 0, 0).astype(BF16)

    def backward(py, pz):
        p_b = py * SIDE + pz
        grad_p = jnp.concatenate([g_z[py, pz], g_y[py, pz]], axis=1)
        for h in range(2):
            hot = hot_recv[p_b, pl.ds(h * 4 * SLOT, 4 * SLOT)]
            rows = dot(hot, grad_p).astype(BF16)
            for k in range(4):
                i = h * 4 + k
                rows_buf[py, pz, i] = dot(
                    a_in[py, pz, i], rows[k * SLOT : (k + 1) * SLOT], 0, 0
                ).astype(BF16)

    backward(y, z)

    def near_first(n, _):
        f_z, f_y = (z + 3 - 2 * n) % SIDE, (y + 3 - 2 * n) % SIDE
        got(0, y, f_z)
        pass_on(0, True, y, f_z, 0, n)
        push(0, False, y, f_z, 2 + n)
        got(1, f_y, z)
        pass_on(1, False, f_y, z, 0, n)
        push(1, True, f_y, z, 2 + n)
        return 0

    def near_second(n, _):
        f_z, f_y = (z + 3 - 2 * n) % SIDE, (y + 3 - 2 * n) % SIDE
        got(1, y, f_z)
        pass_on(1, True, y, f_z, 1, n)
        got(0, f_y, z)
        pass_on(0, False, f_y, z, 1, n)
        return 0

    def near_z(n, _):
        backward(y, (z + 3 - 2 * n) % SIDE)
        return 0

    def near_y(n, _):
        backward((y + 3 - 2 * n) % SIDE, z)
        return 0

    far_y, far_z = (y + 2) % SIDE, (z + 2) % SIDE
    lax.fori_loop(0, 2, near_first, 0)
    lax.fori_loop(0, 2, near_second, 0)
    lax.fori_loop(0, 1, near_z, 0)
    got_parts(0, y, far_z)
    push(0, False, y, far_z, 4)
    got_parts(1, far_y, z)
    push(1, True, far_y, z, 4)

    lax.fori_loop(1, 2, near_z, 0)

    def corners(t, _):
        n, m = t // 2, t % 2
        near, e = 3 - 2 * n, 3 - 2 * m
        got(0, (y + near) % SIDE, (z + e) % SIDE)
        pass_on(0, False, (y + near) % SIDE, (z + e) % SIDE, 2 + m, n)
        got(1, (y + e) % SIDE, (z + near) % SIDE)
        pass_on(1, True, (y + e) % SIDE, (z + near) % SIDE, 2 + m, n)
        return 0

    def edges(n, _):
        near = 3 - 2 * n
        got(0, (y + near) % SIDE, far_z)
        pass_on(0, False, (y + near) % SIDE, far_z, 4, n)
        got(1, far_y, (z + near) % SIDE)
        pass_on(1, True, far_y, (z + near) % SIDE, 4, n)
        return 0

    lax.fori_loop(0, 4, corners, 0)
    lax.fori_loop(0, 2, near_y, 0)
    lax.fori_loop(0, 2, edges, 0)

    def start_w(t, _):
        to = (b + t) % PY
        send(w_term.at[to], w_parts.at[b], s_w.at[t], r_w.at[b], (a, to))
        return 0

    lax.fori_loop(1, PY, start_w, 0)

    def corner(t, _):
        backward((y + 3 - 2 * (t // 2)) % SIDE, (z + 3 - 2 * (t % 2)) % SIDE)
        return 0

    lax.fori_loop(0, 4, corner, 0)

    def edge_z(n, _):
        f_y = (y + 3 - 2 * n) % SIDE
        got_parts(1, f_y, far_z)
        backward(f_y, far_z)
        return 0

    def edge_y(n, _):
        f_z = (z + 3 - 2 * n) % SIDE
        got_parts(0, far_y, f_z)
        backward(far_y, f_z)
        return 0

    got_parts(1, y, far_z)
    backward(y, far_z)
    got_parts(0, far_y, z)
    backward(far_y, z)
    lax.fori_loop(0, 2, edge_z, 0)

    lax.fori_loop(0, 2, edge_y, 0)
    w_sum[a] = w_term[b]

    def add_w(t, _):
        f = (b + t) % PY
        wait(w_parts.at[f], r_w.at[f])
        w_sum[a] = w_sum[a] + w_parts[f]
        return 0

    lax.fori_loop(1, PY, add_w, 0)

    def start_w2(t, _):
        send(w_sum.at[a], w_parts2.at[a], s_w2.at[t], r_w2.at[a], at_px((a + t) % PX))
        return 0

    lax.fori_loop(1, PX, start_w2, 0)

    got_parts(0, far_y, far_z)
    got_parts(1, far_y, far_z)
    backward(far_y, far_z)

    def scatter(i):
        acc = jnp.zeros((ROWS, FEAT), F32)
        for py in range(SIDE):
            index = send_all[i, py]
            hot = jnp.concatenate([hot_columns(index[k : k + 1], 0, ROWS) for k in range(SIDE)], axis=1)
            rows = jnp.concatenate([rows_buf[py, k, i] for k in range(SIDE)], axis=0)
            acc = acc + dot(hot, rows)
        return acc

    def start_core(d, _):
        to_x = (x + d) % SIDE
        bound_core[to_x] = scatter(to_x * CORES + other).astype(BF16)
        send(bound_core.at[to_x], recv_core.at[to_x], s_core.at[d], r_core.at[to_x], at_px(x * CORES + other))
        return 0

    lax.fori_loop(0, SIDE, start_core, 0)

    def start_x(t, _):
        d = (t + 1) % 3 + 1
        to_x = (x + d) % SIDE
        acc = scatter(to_x * CORES + c)
        wait(recv_core.at[to_x], r_core.at[to_x])
        bound_x[to_x] = (acc + recv_core[to_x].astype(F32)).astype(BF16)
        send(bound_x.at[to_x], recv_x.at[x], s_x.at[d], r_x.at[x], at_px(to_x * CORES + c))
        return 0

    lax.fori_loop(0, SIDE - 1, start_x, 0)

    w_parts2[a] = w_sum[a]

    def wait_w2(t, _):
        f = (a + t) % PX
        wait(w_parts2.at[f], r_w2.at[f])
        return 0

    lax.fori_loop(1, PX, wait_w2, 0)
    acc = w_parts2[0]
    for i in range(1, PX):
        acc = acc + w_parts2[i]
    w_all[b] = acc * F32(1.0 / (PX * PY * ROWS) ** 0.5)

    def start_w3(t, _):
        to = (b + t) % PY
        send(w_all.at[b], w_all.at[b], s_w3.at[t], r_w3.at[b], (a, to))
        return 0

    lax.fori_loop(1, PY, start_w3, 0)
    acc = scatter(a)
    wait(recv_core.at[x], r_core.at[x])
    acc = acc + recv_core[x].astype(F32)

    def wait_w3(t, _):
        f = (b + t) % PY
        wait(w_all.at[f], r_w3.at[f])
        return 0

    lax.fori_loop(1, PY, wait_w3, 0)
    weight_grad[...] = w_all[...].reshape(FEAT, FEAT)

    for d in range(1, SIDE):
        f = (x + d) % SIDE
        wait(recv_x.at[f], r_x.at[f])
        acc = acc + recv_x[f].astype(F32)
    bound_grad[...] = acc.astype(BF16)

    def done_px(t, _):
        wait(send_all.at[0], s_sidx.at[t])
        for k in range(SIDE):
            wait(a_out.at[0, 0], s_out.at[t, k])
        wait(w_sum.at[0], s_w2.at[t])
        return 0

    def done_py(t, _):
        wait(recv_all.at[0], s_ridx.at[t])
        wait(w_term.at[0], s_w.at[t])
        wait(w_all.at[0], s_w3.at[t])
        return 0

    def done_in(t, _):
        wait(a_in.at[0, 0], s_in.at[t // SIDE, t % SIDE])
        return 0

    def done_side(d, _):
        wait(stale_all.at[0], s_stale.at[d])
        wait(send_z2.at[0], s_z2.at[d])
        wait(send_y2.at[0], s_y2.at[d])
        wait(bound_x.at[0], s_x.at[d])
        return 0

    def done_core(d, _):
        wait(stale_all.at[0], s_fwd.at[d])
        wait(bound_core.at[0], s_core.at[d])
        return 0

    def done_g(t, _):
        k, n = t // 2, t % 2
        wait(g_z.at[0, 0], s_gz.at[k, n])
        wait(g_y.at[0, 0], s_gy.at[k, n])
        wait(g_z.at[0, 0, pl.ds(0, FEAT)], s_hz.at[k, n])
        wait(g_y.at[0, 0, pl.ds(0, FEAT)], s_hy.at[k, n])
        return 0

    def done_sums(t, _):
        k, n = t // 2, t % 2
        wait(part_z.at[0, 0], s_z.at[k, n])
        wait(part_y.at[0, 0], s_y.at[k, n])
        wait(part_z.at[0, 0, pl.ds(0, FEAT)], s_hz1.at[k, n])
        wait(part_y.at[0, 0, pl.ds(0, FEAT)], s_hy1.at[k, n])
        return 0

    lax.fori_loop(0, 8, done_sums, 0)
    lax.fori_loop(0, 10, done_g, 0)
    lax.fori_loop(1, PX, done_px, 0)
    lax.fori_loop(1, PY, done_py, 0)
    lax.fori_loop(1, PY, done_in, 0)
    lax.fori_loop(1, SIDE, done_side, 0)
    lax.fori_loop(0, SIDE, done_core, 0)


def hand_over(*refs):
    count = len(refs) // 2
    for source, result in zip(refs[:count], refs[count:]):
        result[...] = source[...]


def on_device(
    feats, stale_feats, local_adj, adj_in, adj_out, owner, send_idx, recv_idx, weight, cotangent
):
    hbm = pl.BlockSpec(memory_space=pl.ANY)
    vmem = pl.BlockSpec(memory_space=pltpu.VMEM)
    dma = lambda *shape: pltpu.SemaphoreType.DMA(shape)
    node = lambda *shape: pltpu.VMEM((*shape, ROWS, HALF), BF16)
    shapes = (
        jax.ShapeDtypeStruct((ROWS, FEAT), BF16),
        jax.ShapeDtypeStruct((ROWS, FEAT), BF16),
        jax.ShapeDtypeStruct((ROWS, FEAT), BF16),
        jax.ShapeDtypeStruct((FEAT, FEAT), F32),
    )
    results = pl.pallas_call(
        kernel,
        out_shape=shapes,
        in_specs=[hbm] * 5 + [pl.BlockSpec(memory_space=pltpu.SMEM)] + [vmem] * 4,
        out_specs=(vmem,) * 4,
        scratch_shapes=[
            pltpu.VMEM((SIDE, SIDE, PX, SLOT, SLOT), BF16),
            pltpu.VMEM((PX, SIDE, SIDE, SLOT, SLOT), BF16),
            pltpu.VMEM((PX, ROWS, FEAT), BF16),
            pltpu.VMEM((PX, SIDE, SIDE, SLOT), jnp.int32),
            pltpu.VMEM((PY, PX, SLOT), jnp.int32),
            pltpu.VMEM((SIDE, SIDE, PX, SLOT, FEAT), BF16),
            pltpu.VMEM((PX * SLOT, FEAT), BF16),
            node(SIDE, SIDE),
            node(SIDE, SIDE),
            node(SIDE, 2),
            node(SIDE, 2),
            pltpu.VMEM((SIDE, 2, FEAT, HALF), BF16),
            pltpu.VMEM((SIDE, 2, FEAT, HALF), BF16),
            node(SIDE),
            node(SIDE),
            node(SIDE),
            node(SIDE),
            pltpu.VMEM((ROWS, FEAT), F32),
            node(SIDE, SIDE),
            node(SIDE, SIDE),
            pltpu.VMEM((SIDE, ROWS, FEAT), BF16),
            pltpu.VMEM((SIDE, ROWS, FEAT), BF16),
            pltpu.VMEM((SIDE, ROWS, FEAT), BF16),
            pltpu.VMEM((SIDE, ROWS, FEAT), BF16),
            pltpu.VMEM((PY, PART, FEAT), F32),
            pltpu.VMEM((PY, PART, FEAT), F32),
            pltpu.VMEM((PX, PART, FEAT), F32),
            pltpu.VMEM((PX, PART, FEAT), F32),
            pltpu.VMEM((PY, PART, FEAT), F32),
            pltpu.VMEM((PY, PX * SLOT, ROWS), BF16),
            dma(PY), dma(PY), dma(PX), dma(PX),
            dma(SIDE), dma(PX), dma(SIDE),
            dma(PX, SIDE), dma(PX, SIDE), dma(SIDE, SIDE), dma(SIDE, SIDE),
            dma(SIDE, 2), dma(SIDE, 2), dma(SIDE, 2), dma(SIDE, 2),
            dma(SIDE, 2), dma(SIDE, 2), dma(SIDE, 2), dma(SIDE, 2),
            dma(SIDE), dma(SIDE), dma(SIDE), dma(SIDE),
            dma(SIDE + 1, 2), dma(SIDE, SIDE, 2), dma(SIDE + 1, 2), dma(SIDE, SIDE, 2),
            dma(SIDE + 1, 2), dma(SIDE + 1, 2),
            dma(SIDE), dma(SIDE), dma(SIDE), dma(SIDE),
            dma(PY), dma(PY), dma(PX), dma(PX), dma(PY), dma(PY),
        ],
        compiler_params=pltpu.CompilerParams(
            collective_id=0, has_side_effects=True, vmem_limit_bytes=60 * 2**20
        ),
    )(
        adj_in.reshape(PX, SIDE, SIDE, SLOT, SLOT),
        adj_out.reshape(PX, SIDE, SIDE, SLOT, SLOT),
        stale_feats,
        send_idx.reshape(PX, SIDE, SIDE, SLOT),
        recv_idx.reshape(PX, PY, SLOT),
        owner,
        feats,
        local_adj,
        weight,
        cotangent,
    )
    return pl.pallas_call(
        hand_over, out_shape=shapes, in_specs=[vmem] * 4, out_specs=(vmem,) * 4
    )(*results)


def solution(mesh):
    both = ("px", "py")
    in_specs = (
        P(both, None),
        P(both, None),
        P(both, None),
        P(both, None, None),
        P(both, None, None),
        P(),
        P(both, None),
        P(both, None),
        P(),
        P(both, None),
    )
    out_specs = (P(both, None), P(both, None), P(both, None), P())
    return jax.shard_map(
        on_device, mesh=mesh, in_specs=in_specs, out_specs=out_specs, check_vma=False
    )
```
